32 devices in a mesh: row: 4 (over y, x), rep: 8 (over z, core).
Axes of the slice: x: 2, y: 2, z: 4, core: 2. Of those that a mesh axis runs over, the one named last changes fastest.
Arguments:
- features: bfloat16 [24576, 128], P(('row', 'rep')), may hold values from -6 to 6
- node_order: int32 [32, 768], P(('row', 'rep')), may hold values from 0 to 767, each once within a row
- weight: bfloat16 [128, 128], replicated, may hold values from -0.5 to 0.5
- tile_vals: bfloat16 [192, 8, 4, 128, 128], P('row', 'rep'), may hold values from -0.09375 to 0.09375
- tile_cols: int32 [192, 8, 4], P('row', 'rep'), may hold values from 0 to 23, as said below
- row_counts: int32 [192, 8], P('row', 'rep'), may hold values from 1 to 4
- cotangent: bfloat16 [24576, 128], P(('row', 'rep')), may hold values from -6 to 6
Outputs:
- hidden_out: bfloat16 [24576, 128], P(('row', 'rep'))
- feature_grad: bfloat16 [24576, 128], P(('row', 'rep'))
- weight_grad: float32 [128, 128], replicated
The draws below stay inside these ranges and needn't reach their ends.
Inputs may be any that keep to these rules, and one draw needn't show every extreme that they name: `tile_cols`: within one tile-row and block-column the 4 slots name distinct tile-columns.
All inputs are finite; a program needn't handle non-finite values.
Results may differ from the reference program's by a relative error of at most 0.005.
Values may be sent and summed in bfloat16 or wider, within the bound.
A program may use at most 128 MiB of HBM per device.

```python
import math
import jax
import jax.numpy as jnp
from jax import lax

F = 128
F2 = 128
TILE = 128
TS = 6
MAXT = 4
SLAB = 768
NSLAB = 32
NODES = 24576
NTR = 192
NCT = 24
N_ROW = 4
N_REP = 8


def draw_row_counts(key, part):
    key = jax.random.fold_in(key, 11)
    base_key, block_key = jax.random.split(key)
    base = jax.random.randint(base_key, (NTR, N_REP), 1, MAXT + 1)
    block_cap = jax.random.randint(block_key, (N_ROW, N_REP), 1, MAXT + 1)
    group_index = jnp.arange(NTR) // (N_REP * TS)
    capped = jnp.minimum(base, block_cap[group_index])
    slab_rep = jnp.arange(NTR) // TS % N_REP
    diagonal = slab_rep[:, None] == jnp.arange(N_REP)[None, :]
    return jnp.where(diagonal, MAXT, capped).astype(jnp.int32)


def draw_tile_cols(key, part):
    key = jax.random.fold_in(key, 12)
    row_keys = jax.random.split(key, NTR * N_REP)
    shuffled = jax.vmap(lambda one_key: jax.random.permutation(one_key, NCT))(row_keys)
    return shuffled[:, :MAXT].reshape(NTR, N_REP, MAXT).astype(jnp.int32)


def block_levels(stream_key, dims, cuts, smallest, largest):
    def one(axis_at, shards_of):
        heights = jax.random.uniform(jax.random.fold_in(jax.random.fold_in(stream_key, 6), axis_at), (shards_of,), jnp.float32, smallest / len(cuts), largest / len(cuts))
        return jnp.repeat(jnp.exp(heights), dims[axis_at] // shards_of).reshape((-1,) + (1,) * (len(dims) - axis_at - 1))

    factor_of = one(*cuts[0])
    for cut in cuts[1:]:
        factor_of = factor_of * one(*cut)
    return factor_of


def normal_values(key, dims, scale, limit, cuts=(), kind=jnp.bfloat16):
    loudness = block_levels(key, dims, cuts, -0.22, 0.18) if cuts else 1.0
    drawn = jax.random.normal(key, dims, jnp.float32) * scale * loudness
    return jnp.minimum(jnp.maximum(drawn, -limit), limit).astype(kind)


def setup_inputs(seed: int = 0) -> dict:
    arg_keys = jax.random.split(jax.random.key(seed), 8)
    return {
        "features": normal_values(arg_keys[0], (NODES, F), 1.0, 6.0, ((0, 32),)),
        "node_order": jax.vmap(lambda own: jax.random.permutation(own, SLAB))(jax.random.split(arg_keys[1], NSLAB)).reshape((NSLAB, SLAB)).astype(jnp.int32),
        "weight": normal_values(arg_keys[2], (F, F2), F ** -0.5, 0.5),
        "tile_vals": normal_values(arg_keys[3], (NTR, N_REP, MAXT, TILE, TILE), (N_REP * MAXT * TILE) ** -0.5, 0.09375, ((0, 4), (1, 8))),
        "tile_cols": draw_tile_cols(jax.random.fold_in(arg_keys[7], 71), 0),
        "row_counts": draw_row_counts(jax.random.fold_in(arg_keys[7], 71), 0),
        "cotangent": normal_values(arg_keys[6], (NODES, F2), 1.0, 6.0, ((0, 32),)),
    }


def reference(features, node_order, weight, tile_vals, tile_cols, row_counts, cotangent):
    reordered = jnp.take_along_axis(features.reshape(NSLAB, SLAB, F), node_order[:, :, None].astype(jnp.int32), axis=1).reshape(NODES, F)
    projected = jnp.dot(reordered, weight, preferred_element_type=jnp.float32).astype(jnp.bfloat16)
    section_z = projected.reshape(N_ROW, N_REP, TS, TILE, F2).transpose(1, 0, 2, 3, 4).reshape(N_REP, NCT, TILE, F2)
    rep_index = jnp.arange(N_REP, dtype=jnp.int32)[:, None]
    slot_index = jnp.arange(MAXT, dtype=jnp.int32)

    def forward_row(inputs):
        values, columns, counts = inputs
        picked = section_z[rep_index, columns]
        present = (slot_index[None, :] < counts[:, None]).astype(jnp.float32)
        masked = picked.astype(jnp.float32) * present[:, :, None, None]
        return jnp.einsum('jmab,jmbf->af', values.astype(jnp.float32), masked)
    hidden_out = lax.map(forward_row, (tile_vals, tile_cols, row_counts)).reshape(NODES, F2).astype(jnp.bfloat16)
    grad_rows = cotangent.reshape(NTR, TILE, F2)

    def backward_row(carry, inputs):
        values, columns, counts, grad_tile = inputs
        present = (slot_index[None, :] < counts[:, None]).astype(jnp.float32)
        contrib = jnp.einsum('jmab,af->jmbf', values.astype(jnp.float32), grad_tile.astype(jnp.float32))
        contrib = contrib * present[:, :, None, None]
        return (carry.at[rep_index, columns].add(contrib), None)
    start_grad = jnp.zeros((N_REP, NCT, TILE, F2), jnp.float32)
    stacked, unused = lax.scan(backward_row, start_grad, (tile_vals, tile_cols, row_counts, grad_rows))
    node_grad = stacked.reshape(N_REP, N_ROW, TS, TILE, F2).transpose(1, 0, 2, 3, 4).reshape(NODES, F2).astype(jnp.bfloat16)
    feature_grad = jnp.dot(node_grad, weight.T, preferred_element_type=jnp.float32).astype(jnp.bfloat16)
    weight_grad = jnp.dot(reordered.T, node_grad, preferred_element_type=jnp.float32) * (1.0 / math.sqrt(NODES))
    return (hidden_out, feature_grad, weight_grad)
```

```python
import functools
import math

import jax
import jax.numpy as jnp
from jax import lax
from jax.experimental import pallas as pl
from jax.experimental.pallas import tpu as pltpu
from jax.sharding import PartitionSpec as P

MESH = pl.DeviceIdType.MESH
VMEM_LIMIT = 52 * 1024 * 1024
F32 = jnp.float32
BF16 = jnp.bfloat16


def remote(src, dst, send, recv, device):
    return pltpu.make_async_remote_copy(
        src_ref=src, dst_ref=dst, send_sem=send, recv_sem=recv, device_id=device, device_id_type=MESH
    )


def enter(devices):
    barrier = pltpu.get_barrier_semaphore()
    for device in devices:
        pl.semaphore_signal(barrier, inc=1, device_id=device, device_id_type=MESH)
    pl.semaphore_wait(barrier, len(devices))


def forward_kernel(
    n_row, n_rep, feat, order, weight, cols, counts, cot, vals_hbm,
    x_all, c_all, pair_out,
    vals, z, to_sib, from_sib,
    vals_sem, x_send, x_recv, c_send, c_recv, f_send, f_recv, h_send, h_recv,
):
    row, rep = lax.axis_index("row"), lax.axis_index("rep")
    places = n_rep // 2
    core, place = lax.rem(rep, 2), rep // 2
    slab = feat.shape[0]
    tile = z.shape[1]
    per_slab = slab // tile
    slots = cols.shape[2]
    sibling = (row, place * 2 + 1 - core)
    row_peers = [(lax.rem(row + d, n_row), rep) for d in range(1, n_row)]
    rep_peers = [(row, lax.rem(place + d, places) * 2 + core) for d in range(1, places)]
    load = pltpu.make_async_copy(vals_hbm, vals, vals_sem)
    load.start()
    enter([sibling] + row_peers + rep_peers)

    started = []
    for d, peer in enumerate(rep_peers, 1):
        copy = remote(cot, c_all.at[rep], c_send.at[d], c_recv.at[d], peer)
        copy.start()
        started.append(copy)
    own_to_sib = remote(cot, c_all.at[rep], f_send.at[0], f_recv.at[0], sibling)
    own_to_sib.start()
    started.append(own_to_sib)
    c_all[rep] = cot[...]

    lane = lax.broadcasted_iota(jnp.int32, (tile, slab), 1)
    for t in range(per_slab):
        piece = order[0:1, t * tile : (t + 1) * tile]
        column = jnp.transpose(jnp.broadcast_to(piece, (tile, tile)))
        wide = jnp.concatenate([column] * per_slab, axis=1)
        pick = jnp.where(wide == lane, 1.0, 0.0).astype(BF16)
        x_all[row, pl.ds(t * tile, tile), :] = jnp.dot(
            pick, feat[...], preferred_element_type=F32
        ).astype(BF16)
    x_copies = []
    for d, peer in enumerate(row_peers, 1):
        copy = remote(x_all.at[row], x_all.at[row], x_send.at[d], x_recv.at[d], peer)
        copy.start()
        x_copies.append(copy)
    started.extend(x_copies)

    def project(owner):
        for t in range(per_slab):
            z[owner * per_slab + t] = jnp.dot(
                x_all[owner, pl.ds(t * tile, tile), :], weight[...], preferred_element_type=F32
            ).astype(BF16)

    z[n_row * per_slab] = jnp.zeros((tile, z.shape[2]), BF16)
    project(row)
    for d in range(1, n_row):
        sender = lax.rem(row - d + n_row, n_row)
        remote(
            x_all.at[sender], x_all.at[sender], x_send.at[d], x_recv.at[d], (sender, rep)
        ).wait_recv()
        project(sender)
    load.wait()

    def block_row(r):
        count = counts[r, 0]
        left = jnp.concatenate([vals[r, m] for m in range(slots)], axis=1)
        picked = [
            z[jnp.where(m < count, cols[r, 0, m], n_row * per_slab)] for m in range(slots)
        ]
        return jnp.dot(left, jnp.concatenate(picked, axis=0), preferred_element_type=F32)

    def for_sibling(q, carry):
        first = (q * 2 + 1 - core) * per_slab
        for t in range(per_slab):
            to_sib[q, pl.ds(t * tile, tile), :] = block_row(first + t).astype(BF16)
        remote(to_sib.at[q], from_sib.at[q], h_send.at[q], h_recv.at[q], sibling).start()
        return carry

    lax.fori_loop(0, places, for_sibling, 0)

    def for_self(q, carry):
        first = (q * 2 + core) * per_slab
        remote(to_sib.at[q], from_sib.at[q], h_send.at[q], h_recv.at[q], sibling).wait()
        for t in range(per_slab):
            rows = pl.ds(t * tile, tile)
            pair_out[q, rows, :] = (block_row(first + t) + from_sib[q, rows, :].astype(F32)).astype(BF16)
        return carry

    lax.fori_loop(0, places, for_self, 0)

    for d in range(1, places):
        sender = lax.rem(place - d + places, places) * 2 + core
        remote(
            c_all.at[sender], c_all.at[sender], c_send.at[d], c_recv.at[d], (row, sender)
        ).wait_recv()
        copy = remote(c_all.at[sender], c_all.at[sender], f_send.at[d], f_recv.at[d], sibling)
        copy.start()
        started.append(copy)
    for d in range(places):
        origin = lax.rem(place - d + places, places) * 2 + 1 - core
        remote(
            c_all.at[origin], c_all.at[origin], f_send.at[d], f_recv.at[d], sibling
        ).wait_recv()
    for copy in started:
        copy.wait_send()


def backward_kernel(cols, counts, vals, cot, x_all, spread, local, total):
    step = pl.program_id(0)
    rows, slots, tile = vals.shape[0], vals.shape[1], vals.shape[2]
    tiles = total.shape[0] - 1

    @pl.when(step == 0)
    def _():
        total[...] = jnp.zeros_like(total)

    for k in range(rows):
        r = step * rows + k
        count = counts[r, 0]
        wide = jnp.concatenate([vals[k, m] for m in range(slots)], axis=1)
        terms = lax.dot_general(
            cot[k], wide, (((0,), (0,)), ((), ())), preferred_element_type=F32
        )
        for m in range(slots):
            at = jnp.where(m < count, cols[r, 0, m], tiles)
            total[at] = total[at] + terms[:, m * tile : (m + 1) * tile]

    @pl.when(step == pl.num_programs(0) - 1)
    def _():
        acc = jnp.zeros(local.shape, F32)
        for c in range(tiles):
            at = pl.ds(c * tile, tile)
            held = total[c]
            spread[at, :] = jnp.transpose(held).astype(BF16)
            acc += jnp.dot(held.astype(BF16), x_all[at, :], preferred_element_type=F32)
        local[...] = jnp.transpose(acc)


def reduce_kernel(
    n_row, n_rep, scale, pair, spread, local, weight,
    hidden, feature_grad, weight_grad,
    h_in, s_in, w_in, w_row,
    h_send, h_recv, s_send, s_recv, a_send, a_recv, b_send, b_recv, g_send, g_recv,
):
    row, rep = lax.axis_index("row"), lax.axis_index("rep")
    places = n_rep // 2
    core, place = lax.rem(rep, 2), rep // 2
    part = local.shape[0] // n_rep
    row_peers = [(lax.rem(row + d, n_row), rep) for d in range(1, n_row)]
    all_peers = [(row, lax.rem(rep + d, n_rep)) for d in range(1, n_rep)]
    enter(row_peers + all_peers)

    def piece(index):
        return pl.ds(pl.multiple_of(index * part, part), part)

    started = []

    def send(src, dst, send_sem, recv_sem, peer):
        copy = remote(src, dst, send_sem, recv_sem, peer)
        copy.start()
        started.append(copy)

    for d, peer in enumerate(all_peers, 1):
        send(local.at[piece(peer[1])], w_in.at[rep], a_send.at[d], a_recv.at[d], peer)
    for d, peer in enumerate(row_peers, 1):
        send(spread.at[peer[0]], s_in.at[row], s_send.at[d], s_recv.at[d], peer)
    for d in range(1, places):
        other = lax.rem(place + d, places)
        send(pair.at[other], h_in.at[place], h_send.at[d], h_recv.at[d], (row, other * 2 + core))

    w_in[rep] = local[piece(rep), :]
    for d in range(1, n_rep):
        sender = lax.rem(rep - d + n_rep, n_rep)
        remote(
            local.at[piece(rep)], w_in.at[sender], a_send.at[d], a_recv.at[d], (row, sender)
        ).wait_recv()
    w_row[row] = jnp.sum(w_in[...], axis=0)
    for d, peer in enumerate(row_peers, 1):
        send(w_row.at[row], w_row.at[row], b_send.at[d], b_recv.at[d], peer)
    for d in range(1, n_row):
        sender = lax.rem(row - d + n_row, n_row)
        remote(
            w_row.at[sender], w_row.at[sender], b_send.at[d], b_recv.at[d], (sender, rep)
        ).wait_recv()
    weight_grad[piece(rep), :] = jnp.sum(w_row[...], axis=0) * scale
    for d, peer in enumerate(all_peers, 1):
        send(
            weight_grad.at[piece(rep)], weight_grad.at[piece(rep)], g_send.at[d], g_recv.at[d], peer
        )

    grad = spread[row].astype(F32)
    for d in range(1, n_row):
        sender = lax.rem(row - d + n_row, n_row)
        remote(
            spread.at[row], s_in.at[sender], s_send.at[d], s_recv.at[d], (sender, rep)
        ).wait_recv()
        grad += s_in[sender].astype(F32)
    feature_grad[...] = lax.dot_general(
        grad.astype(BF16), weight[...], (((1,), (1,)), ((), ())), preferred_element_type=F32
    ).astype(BF16)

    rows = pair[place].astype(F32)
    for d in range(1, places):
        sender = lax.rem(place - d + places, places)
        remote(
            pair.at[place], h_in.at[sender], h_send.at[d], h_recv.at[d], (row, sender * 2 + core)
        ).wait_recv()
        rows += h_in[sender].astype(F32)
    hidden[...] = rows.astype(BF16)
    for d in range(1, n_rep):
        sender = lax.rem(rep - d + n_rep, n_rep)
        remote(
            weight_grad.at[piece(sender)], weight_grad.at[piece(sender)],
            g_send.at[d], g_recv.at[d], (row, sender),
        ).wait_recv()
    for copy in started:
        copy.wait_send()


def solution(mesh):
    n_row, n_rep = mesh.shape["row"], mesh.shape["rep"]
    places = n_rep // 2
    vmem = pl.BlockSpec(memory_space=pltpu.VMEM)
    smem = pl.BlockSpec(memory_space=pltpu.SMEM)
    dma = pltpu.SemaphoreType.DMA

    def shards(features, node_order, weight, tile_vals, tile_cols, row_counts, cotangent):
        slab, width = features.shape
        depth = weight.shape[1]
        tile_rows, _, slots, tile, _ = tile_vals.shape
        tiles = n_row * slab // tile
        vals = tile_vals.reshape(tile_rows, slots, tile, tile)
        shape = jax.ShapeDtypeStruct
        x_all, c_all, pair = pl.pallas_call(
            functools.partial(forward_kernel, n_row, n_rep),
            name="forward",
            out_shape=(
                shape((n_row, slab, width), BF16),
                shape((n_rep, slab, depth), BF16),
                shape((places, slab, depth), BF16),
            ),
            in_specs=[vmem, vmem, vmem, smem, smem, vmem, pl.BlockSpec(memory_space=pl.ANY)],
            out_specs=(vmem, vmem, vmem),
            scratch_shapes=[
                pltpu.VMEM(vals.shape, BF16),
                pltpu.VMEM((tiles + 1, tile, depth), BF16),
                pltpu.VMEM((places, slab, depth), BF16),
                pltpu.VMEM((places, slab, depth), BF16),
                dma,
                dma((n_row,)), dma((n_row,)),
                dma((places,)), dma((places,)),
                dma((places,)), dma((places,)),
                dma((places,)), dma((places,)),
            ],
            compiler_params=pltpu.CompilerParams(
                collective_id=0, has_side_effects=True, vmem_limit_bytes=VMEM_LIMIT
            ),
        )(features, node_order, weight, tile_cols, row_counts, cotangent, vals)

        chunk = 8
        spread, local = pl.pallas_call(
            backward_kernel,
            name="backward",
            grid=(tile_rows // chunk,),
            out_shape=(shape((tiles * tile, depth), BF16), shape((width, depth), F32)),
            in_specs=[
                smem, smem,
                pl.BlockSpec((chunk, slots, tile, tile), lambda i: (i, 0, 0, 0)),
                pl.BlockSpec((chunk, tile, depth), lambda i: (i, 0, 0)),
                pl.BlockSpec((tiles * tile, width), lambda i: (0, 0)),
            ],
            out_specs=(
                pl.BlockSpec((tiles * tile, depth), lambda i: (0, 0)),
                pl.BlockSpec((width, depth), lambda i: (0, 0)),
            ),
            scratch_shapes=[pltpu.VMEM((tiles + 1, depth, tile), F32)],
            compiler_params=pltpu.CompilerParams(vmem_limit_bytes=VMEM_LIMIT),
        )(
            tile_cols, row_counts, vals,
            c_all.reshape(tile_rows, tile, depth), x_all.reshape(tiles * tile, width),
        )

        nodes = slab * n_row * n_rep
        part = width // n_rep
        return pl.pallas_call(
            functools.partial(reduce_kernel, n_row, n_rep, 1.0 / math.sqrt(nodes)),
            name="reduce",
            out_shape=(
                shape((slab, depth), BF16),
                shape((slab, width), BF16),
                shape((width, depth), F32),
            ),
            in_specs=[vmem] * 4,
            out_specs=(vmem,) * 3,
            scratch_shapes=[
                pltpu.VMEM((places, slab, depth), BF16),
                pltpu.VMEM((n_row, slab, depth), BF16),
                pltpu.VMEM((n_rep, part, depth), F32),
                pltpu.VMEM((n_row, part, depth), F32),
                dma((places,)), dma((places,)),
                dma((n_row,)), dma((n_row,)),
                dma((n_rep,)), dma((n_rep,)),
                dma((n_row,)), dma((n_row,)),
                dma((n_rep,)), dma((n_rep,)),
            ],
            compiler_params=pltpu.CompilerParams(
                collective_id=1, has_side_effects=True, vmem_limit_bytes=VMEM_LIMIT
            ),
        )(pair, spread.reshape(n_row, slab, depth), local, weight)

    return jax.shard_map(
        shards,
        mesh=mesh,
        in_specs=(
            P(("row", "rep"), None),
            P(("row", "rep"), None),
            P(),
            P("row", "rep", None, None, None),
            P("row", "rep", None),
            P("row", "rep"),
            P(("row", "rep"), None),
        ),
        out_specs=(P(("row", "rep"), None), P(("row", "rep"), None), P()),
        check_vma=False,
    )
```

```python
import functools
import math

import jax
import jax.numpy as jnp
from jax import lax
from jax.experimental import pallas as pl
from jax.experimental.pallas import tpu as pltpu
from jax.sharding import PartitionSpec as P

MESH = pl.DeviceIdType.MESH
VMEM_LIMIT = 63 * 1024 * 1024
F32 = jnp.float32
BF16 = jnp.bfloat16
HALVES = 2


def remote(src, dst, send, recv, device):
    return pltpu.make_async_remote_copy(
        src_ref=src, dst_ref=dst, send_sem=send, recv_sem=recv, device_id=device, device_id_type=MESH
    )


def enter(devices):
    barrier = pltpu.get_barrier_semaphore()
    for device in devices:
        pl.semaphore_signal(barrier, inc=1, device_id=device, device_id_type=MESH)
    pl.semaphore_wait(barrier, len(devices))


def forward_kernel(
    n_row, n_rep, feat_hbm, order_hbm, weight_hbm, cols, counts, cot, vals_hbm,
    x_all, c_all, pair_out,
    vals, feat, order, weight, z, to_sib, from_sib,
    load_sem, x_send, x_recv, r_send, r_recv, l_send, l_recv, f_send, f_recv, h_send, h_recv, p_sem,
):
    row, rep = lax.axis_index("row"), lax.axis_index("rep")
    places = n_rep // 2
    core, place = lax.rem(rep, 2), rep // 2
    slab = feat.shape[0]
    half = slab // HALVES
    tile = z.shape[1]
    per_slab = slab // tile
    slots = cols.shape[1]
    sibling = (row, place * 2 + 1 - core)
    row_peers = [(lax.rem(row + d, n_row), rep) for d in range(1, n_row)]
    right = (row, lax.rem(place + 1, places) * 2 + core)
    left = (row, lax.rem(place + places - 1, places) * 2 + core)
    loads = [
        pltpu.make_async_copy(src, dst, load_sem.at[i])
        for i, (src, dst) in enumerate(
            [(feat_hbm, feat), (order_hbm, order), (weight_hbm, weight), (vals_hbm, vals), (cot, c_all.at[rep])]
        )
    ]
    for load in loads:
        load.start()
    enter([sibling, left, right] + row_peers)

    def block(index, h):
        return c_all.at[index, pl.ds(h * half, half)]

    for h in range(HALVES):
        own = cot.at[pl.ds(h * half, half)]

        @pl.when(place < places - 1)
        def _():
            remote(own, block(rep, h), r_send.at[0, h], r_recv.at[0, h], right).start()

        @pl.when(place > 0)
        def _():
            remote(own, block(rep, h), l_send.at[0, h], l_recv.at[0, h], left).start()

    for h in range(HALVES):
        own = cot.at[pl.ds(h * half, half)]
        remote(own, block(rep, h), f_send.at[place, h], f_recv.at[place, h], sibling).start()

    def relay(step):
        for h in range(HALVES):

            @pl.when(place >= step)
            def _():
                origin = place - step
                held = block(origin * 2 + core, h)
                remote(held, held, r_send.at[step - 1, h], r_recv.at[step - 1, h], left).wait_recv()
                if step < places - 1:

                    @pl.when(place < places - 1)
                    def _():
                        remote(held, held, r_send.at[step, h], r_recv.at[step, h], right).start()

                remote(held, held, f_send.at[origin, h], f_recv.at[origin, h], sibling).start()

            @pl.when(place + step < places)
            def _():
                origin = place + step
                held = block(origin * 2 + core, h)
                remote(held, held, l_send.at[step - 1, h], l_recv.at[step - 1, h], right).wait_recv()
                if step < places - 1:

                    @pl.when(place > 0)
                    def _():
                        remote(held, held, l_send.at[step, h], l_recv.at[step, h], left).start()

                remote(held, held, f_send.at[origin, h], f_recv.at[origin, h], sibling).start()

    for load in loads[:3]:
        load.wait()
    lane = lax.broadcasted_iota(jnp.int32, (tile, slab), 1)
    for t in range(per_slab):
        piece = order[0:1, t * tile : (t + 1) * tile]
        column = jnp.transpose(jnp.broadcast_to(piece, (tile, tile)))
        wide = jnp.concatenate([column] * per_slab, axis=1)
        pick = jnp.where(wide == lane, 1.0, 0.0).astype(BF16)
        x_all[row, pl.ds(t * tile, tile), :] = jnp.dot(
            pick, feat[...], preferred_element_type=F32
        ).astype(BF16)
    x_copies = []
    for d, peer in enumerate(row_peers, 1):
        copy = remote(x_all.at[row], x_all.at[row], x_send.at[d], x_recv.at[d], peer)
        copy.start()
        x_copies.append(copy)

    def project(owner):
        for t in range(per_slab):
            z[owner * per_slab + t] = jnp.dot(
                x_all[owner, pl.ds(t * tile, tile), :], weight[...], preferred_element_type=F32
            ).astype(BF16)

    z[n_row * per_slab] = jnp.zeros((tile, z.shape[2]), BF16)
    project(row)
    for d in range(1, n_row):
        sender = lax.rem(row - d + n_row, n_row)
        remote(
            x_all.at[sender], x_all.at[sender], x_send.at[d], x_recv.at[d], (sender, rep)
        ).wait_recv()
        project(sender)
    loads[3].wait()
    relay(1)

    def block_row(r):
        count = counts[0, r]
        lhs = jnp.concatenate([vals[r, m] for m in range(slots)], axis=1)
        picked = [
            z[jnp.where(m < count, cols[0, m, r], n_row * per_slab)] for m in range(slots)
        ]
        return jnp.dot(lhs, jnp.concatenate(picked, axis=0), preferred_element_type=F32)

    def for_sibling(q, carry):
        first = (q * 2 + 1 - core) * per_slab
        for t in range(per_slab):
            to_sib[q, pl.ds(t * tile, tile), :] = block_row(first + t).astype(BF16)
        remote(to_sib.at[q], from_sib.at[q], h_send.at[q], h_recv.at[q], sibling).start()
        return carry

    lax.fori_loop(0, places, for_sibling, 0)
    if places > 2:
        relay(2)

    def for_self(q, carry):
        first = (q * 2 + core) * per_slab
        remote(to_sib.at[q], from_sib.at[q], h_send.at[q], h_recv.at[q], sibling).wait()
        for t in range(per_slab):
            rows = pl.ds(t * tile, tile)
            from_sib[q, rows, :] = (block_row(first + t) + from_sib[q, rows, :].astype(F32)).astype(BF16)
        pltpu.make_async_copy(from_sib.at[q], pair_out.at[q], p_sem.at[q]).start()
        return carry

    lax.fori_loop(0, places, for_self, 0)

    for step in range(3, places):
        relay(step)

    for q in range(places):
        pltpu.make_async_copy(from_sib.at[q], pair_out.at[q], p_sem.at[q]).wait()
        for h in range(HALVES):
            held = block(q * 2 + 1 - core, h)
            remote(held, held, f_send.at[q, h], f_recv.at[q, h], sibling).wait()
    loads[4].wait()
    for copy in x_copies:
        copy.wait_send()
    for step in range(places - 1):
        for h in range(HALVES):
            held = block(rep, h)

            @pl.when((place < places - 1) & (place >= step))
            def _():
                remote(held, held, r_send.at[step, h], r_recv.at[step, h], right).wait_send()

            @pl.when((place > 0) & (place + step < places))
            def _():
                remote(held, held, l_send.at[step, h], l_recv.at[step, h], left).wait_send()


def backward_kernel(cols, counts, vals, cot, x_all, spread, local, total):
    step = pl.program_id(0)
    rows, slots, tile = vals.shape[0], vals.shape[1], vals.shape[2]
    tiles = total.shape[0] - 1

    @pl.when(step == 0)
    def _():
        total[...] = jnp.zeros_like(total)

    for k in range(rows):
        r = step * rows + k
        count = counts[0, r]
        wide = jnp.concatenate([vals[k, m] for m in range(slots)], axis=1)
        terms = lax.dot_general(
            cot[k], wide, (((0,), (0,)), ((), ())), preferred_element_type=F32
        )
        for m in range(slots):
            at = jnp.where(m < count, cols[0, m, r], tiles)
            total[at] = total[at] + terms[:, m * tile : (m + 1) * tile]

    @pl.when(step == pl.num_programs(0) - 1)
    def _():
        acc = jnp.zeros(local.shape, F32)
        for c in range(tiles):
            at = pl.ds(c * tile, tile)
            held = total[c]
            spread[at, :] = jnp.transpose(held).astype(BF16)
            acc += jnp.dot(held.astype(BF16), x_all[at, :], preferred_element_type=F32)
        local[...] = jnp.transpose(acc)


def reduce_kernel(
    n_row, n_rep, scale, pair_hbm, spread, local, weight,
    hidden, feature_grad, weight_grad,
    pair, r_in, l_in, r_sum, l_sum, s_in, w_in, w_row,
    r_send, r_recv, l_send, l_recv, own_sem, s_send, s_recv, a_send, a_recv, b_send, b_recv, g_send, g_recv,
):
    row, rep = lax.axis_index("row"), lax.axis_index("rep")
    places = n_rep // 2
    core, place = lax.rem(rep, 2), rep // 2
    part = local.shape[0] // n_rep
    row_peers = [(lax.rem(row + d, n_row), rep) for d in range(1, n_row)]
    all_peers = [(row, lax.rem(rep + d, n_rep)) for d in range(1, n_rep)]
    right = (row, lax.rem(place + 1, places) * 2 + core)
    left = (row, lax.rem(place + places - 1, places) * 2 + core)
    half = pair.shape[1] // HALVES
    own = pltpu.make_async_copy(spread.at[row], s_in.at[row], own_sem.at[0])
    own.start()
    load = pltpu.make_async_copy(pair_hbm, pair, own_sem.at[1])
    load.start()
    enter(row_peers + all_peers)

    def piece(index):
        return pl.ds(pl.multiple_of(index * part, part), part)

    started = []

    def send(src, dst, send_sem, recv_sem, peer):
        copy = remote(src, dst, send_sem, recv_sem, peer)
        copy.start()
        started.append(copy)

    for d, peer in enumerate(all_peers, 1):
        send(local.at[piece(peer[1])], w_in.at[rep], a_send.at[d], a_recv.at[d], peer)
    for d, peer in enumerate(row_peers, 1):
        send(spread.at[peer[0]], s_in.at[row], s_send.at[d], s_recv.at[d], peer)
    def add(held, arrived, q, rows):
        held[q, rows, :] = (arrived[q, rows, :].astype(F32) + pair[q, rows, :].astype(F32)).astype(BF16)

    def relay(step):
        to_right = places - 1 + place - step
        to_left = step - (places - 1) + place
        for h in range(HALVES):
            rows = pl.ds(h * half, half)

            @pl.when((to_right > place) & (to_right < places))
            def _():
                q = to_right
                target, sems = r_in.at[q, rows], (r_send.at[q, h], r_recv.at[q, h])

                @pl.when(place == 0)
                def _():
                    remote(pair.at[q, rows], target, *sems, right).start()

                @pl.when(place > 0)
                def _():
                    remote(target, target, *sems, left).wait_recv()
                    add(r_sum, r_in, q, rows)
                    remote(r_sum.at[q, rows], target, *sems, right).start()

            @pl.when((to_left >= 0) & (to_left < place))
            def _():
                q = to_left
                target, sems = l_in.at[q, rows], (l_send.at[q, h], l_recv.at[q, h])

                @pl.when(place == places - 1)
                def _():
                    remote(pair.at[q, rows], target, *sems, left).start()

                @pl.when(place < places - 1)
                def _():
                    remote(target, target, *sems, right).wait_recv()
                    add(l_sum, l_in, q, rows)
                    remote(l_sum.at[q, rows], target, *sems, left).start()

    load.wait()
    relay(0)
    w_in[rep] = local[piece(rep), :]
    for d in range(1, n_rep):
        sender = lax.rem(rep - d + n_rep, n_rep)
        remote(
            local.at[piece(rep)], w_in.at[sender], a_send.at[d], a_recv.at[d], (row, sender)
        ).wait_recv()
    w_row[row] = jnp.sum(w_in[...], axis=0)
    for d, peer in enumerate(row_peers, 1):
        send(w_row.at[row], w_row.at[row], b_send.at[d], b_recv.at[d], peer)
    for d in range(1, n_row):
        sender = lax.rem(row - d + n_row, n_row)
        remote(
            w_row.at[sender], w_row.at[sender], b_send.at[d], b_recv.at[d], (sender, rep)
        ).wait_recv()
    if places > 2:
        relay(1)
    weight_grad[piece(rep), :] = jnp.sum(w_row[...], axis=0) * scale
    for d, peer in enumerate(all_peers, 1):
        send(
            weight_grad.at[piece(rep)], weight_grad.at[piece(rep)], g_send.at[d], g_recv.at[d], peer
        )

    own.wait()
    grad = s_in[row].astype(F32)
    for d in range(1, n_row):
        sender = lax.rem(row - d + n_row, n_row)
        remote(
            spread.at[row], s_in.at[sender], s_send.at[d], s_recv.at[d], (sender, rep)
        ).wait_recv()
        grad += s_in[sender].astype(F32)
    feature_grad[...] = lax.dot_general(
        grad.astype(BF16), weight[...], (((1,), (1,)), ((), ())), preferred_element_type=F32
    ).astype(BF16)

    for step in range(2, places - 1):
        relay(step)
    for h in range(HALVES):
        rows = pl.ds(h * half, half)

        @pl.when(place > 0)
        def _():
            target = r_in.at[place, rows]
            remote(target, target, r_send.at[place, h], r_recv.at[place, h], left).wait_recv()

        @pl.when(place < places - 1)
        def _():
            target = l_in.at[place, rows]
            remote(target, target, l_send.at[place, h], l_recv.at[place, h], right).wait_recv()

        @pl.when(place == 0)
        def _():
            hidden[rows, :] = (pair[place, rows, :].astype(F32) + l_in[place, rows, :].astype(F32)).astype(BF16)

        @pl.when(place == places - 1)
        def _():
            hidden[rows, :] = (pair[place, rows, :].astype(F32) + r_in[place, rows, :].astype(F32)).astype(BF16)

        @pl.when((place > 0) & (place < places - 1))
        def _():
            hidden[rows, :] = (
                pair[place, rows, :].astype(F32)
                + r_in[place, rows, :].astype(F32)
                + l_in[place, rows, :].astype(F32)
            ).astype(BF16)

    for q in range(places):
        for h in range(HALVES):
            held = r_sum.at[q, pl.ds(h * half, half)]

            @pl.when(place < q)
            def _():
                remote(held, held, r_send.at[q, h], r_recv.at[q, h], right).wait_send()

            @pl.when(place > q)
            def _():
                remote(held, held, l_send.at[q, h], l_recv.at[q, h], left).wait_send()

    for d in range(1, n_rep):
        sender = lax.rem(rep - d + n_rep, n_rep)
        remote(
            weight_grad.at[piece(sender)], weight_grad.at[piece(sender)],
            g_send.at[d], g_recv.at[d], (row, sender),
        ).wait_recv()
    for copy in started:
        copy.wait_send()


def solution(mesh):
    n_row, n_rep = mesh.shape["row"], mesh.shape["rep"]
    places = n_rep // 2
    vmem = pl.BlockSpec(memory_space=pltpu.VMEM)
    smem = pl.BlockSpec(memory_space=pltpu.SMEM)
    hbm = pl.BlockSpec(memory_space=pltpu.HBM)
    dma = pltpu.SemaphoreType.DMA

    def shards(features, node_order, weight, tile_vals, tile_cols, row_counts, cotangent):
        slab, width = features.shape
        depth = weight.shape[1]
        tile_rows, _, slots, tile, _ = tile_vals.shape
        tiles = n_row * slab // tile
        vals = tile_vals.reshape(tile_rows, slots, tile, tile)
        cols = jnp.transpose(tile_cols, (1, 2, 0))
        counts = jnp.transpose(row_counts, (1, 0))
        shape = jax.ShapeDtypeStruct
        x_all, c_all, pair = pl.pallas_call(
            functools.partial(forward_kernel, n_row, n_rep),
            name="forward",
            out_shape=(
                shape((n_row, slab, width), BF16),
                shape((n_rep, slab, depth), BF16),
                shape((places, slab, depth), BF16),
            ),
            in_specs=[hbm, hbm, hbm, smem, smem, hbm, hbm],
            out_specs=(vmem, hbm, hbm),
            scratch_shapes=[
                pltpu.VMEM(vals.shape, BF16),
                pltpu.VMEM(features.shape, BF16),
                pltpu.VMEM(node_order.shape, jnp.int32),
                pltpu.VMEM(weight.shape, BF16),
                pltpu.VMEM((tiles + 1, tile, depth), BF16),
                pltpu.VMEM((places, slab, depth), BF16),
                pltpu.VMEM((places, slab, depth), BF16),
                dma((5,)),
                dma((n_row,)), dma((n_row,)),
                dma((places, HALVES)), dma((places, HALVES)),
                dma((places, HALVES)), dma((places, HALVES)),
                dma((places, HALVES)), dma((places, HALVES)),
                dma((places,)), dma((places,)),
                dma((places,)),
            ],
            compiler_params=pltpu.CompilerParams(
                collective_id=0, has_side_effects=True, vmem_limit_bytes=VMEM_LIMIT
            ),
        )(features, node_order, weight, cols, counts, cotangent, vals)

        chunk = 8
        spread, local = pl.pallas_call(
            backward_kernel,
            name="backward",
            grid=(tile_rows // chunk,),
            out_shape=(shape((tiles * tile, depth), BF16), shape((width, depth), F32)),
            in_specs=[
                smem, smem,
                pl.BlockSpec((chunk, slots, tile, tile), lambda i: (i, 0, 0, 0)),
                pl.BlockSpec((chunk, tile, depth), lambda i: (i, 0, 0)),
                pl.BlockSpec((tiles * tile, width), lambda i: (0, 0)),
            ],
            out_specs=(
                pl.BlockSpec((tiles * tile, depth), lambda i: (0, 0)),
                pl.BlockSpec((width, depth), lambda i: (0, 0)),
            ),
            scratch_shapes=[pltpu.VMEM((tiles + 1, depth, tile), F32)],
            compiler_params=pltpu.CompilerParams(vmem_limit_bytes=VMEM_LIMIT),
        )(
            cols, counts, vals,
            c_all.reshape(tile_rows, tile, depth), x_all.reshape(tiles * tile, width),
        )

        nodes = slab * n_row * n_rep
        part = width // n_rep
        return pl.pallas_call(
            functools.partial(reduce_kernel, n_row, n_rep, 1.0 / math.sqrt(nodes)),
            name="reduce",
            out_shape=(
                shape((slab, depth), BF16),
                shape((slab, width), BF16),
                shape((width, depth), F32),
            ),
            in_specs=[hbm, hbm, vmem, vmem],
            out_specs=(vmem,) * 3,
            scratch_shapes=[
                pltpu.VMEM((places, slab, depth), BF16),
                pltpu.VMEM((places, slab, depth), BF16),
                pltpu.VMEM((places, slab, depth), BF16),
                pltpu.VMEM((places, slab, depth), BF16),
                pltpu.VMEM((places, slab, depth), BF16),
                pltpu.VMEM((n_row, slab, depth), BF16),
                pltpu.VMEM((n_rep, part, depth), F32),
                pltpu.VMEM((n_row, part, depth), F32),
                dma((places, HALVES)), dma((places, HALVES)),
                dma((places, HALVES)), dma((places, HALVES)),
                dma((2,)),
                dma((n_row,)), dma((n_row,)),
                dma((n_rep,)), dma((n_rep,)),
                dma((n_row,)), dma((n_row,)),
                dma((n_rep,)), dma((n_rep,)),
            ],
            compiler_params=pltpu.CompilerParams(
                collective_id=1, has_side_effects=True, vmem_limit_bytes=VMEM_LIMIT
            ),
        )(pair, spread.reshape(n_row, slab, depth), local, weight)

    return jax.shard_map(
        shards,
        mesh=mesh,
        in_specs=(
            P(("row", "rep"), None),
            P(("row", "rep"), None),
            P(),
            P("row", "rep", None, None, None),
            P("row", "rep", None),
            P("row", "rep"),
            P(("row", "rep"), None),
        ),
        out_specs=(P(("row", "rep"), None), P(("row", "rep"), None), P()),
        check_vma=False,
    )
```

```python
import functools
import math

import jax
import jax.numpy as jnp
from jax import lax
from jax.experimental import pallas as pl
from jax.experimental.pallas import tpu as pltpu
from jax.sharding import PartitionSpec as P

MESH = pl.DeviceIdType.MESH
VMEM_LIMIT = 63 * 1024 * 1024
F32 = jnp.float32
BF16 = jnp.bfloat16
MIDDLE_LIMIT = 63 * 1024 * 1024
LATER_LIMIT = 40 * 1024 * 1024
HALVES = 2


def remote(src, dst, send, recv, device):
    return pltpu.make_async_remote_copy(
        src_ref=src, dst_ref=dst, send_sem=send, recv_sem=recv, device_id=device, device_id_type=MESH
    )


def enter(devices):
    barrier = pltpu.get_barrier_semaphore()
    for device in devices:
        pl.semaphore_signal(barrier, inc=1, device_id=device, device_id_type=MESH)
    pl.semaphore_wait(barrier, len(devices))


def forward_kernel(
    n_row, n_rep, feat_hbm, order_hbm, weight_hbm, cols, counts, cot, vals_hbm,
    x_all, c_all, pair_out,
    vals, feat, order, weight, z, to_sib, from_sib,
    load_sem, x_send, x_recv, r_send, r_recv, l_send, l_recv, f_send, f_recv, h_send, h_recv, p_sem,
):
    row, rep = lax.axis_index("row"), lax.axis_index("rep")
    places = n_rep // 2
    core, place = lax.rem(rep, 2), rep // 2
    slab = feat.shape[0]
    half = slab // HALVES
    tile = z.shape[1]
    per_slab = slab // tile
    slots = cols.shape[1]
    sibling = (row, place * 2 + 1 - core)
    row_peers = [(lax.rem(row + d, n_row), rep) for d in range(1, n_row)]
    right = (row, lax.rem(place + 1, places) * 2 + core)
    left = (row, lax.rem(place + places - 1, places) * 2 + core)
    loads = [
        pltpu.make_async_copy(src, dst, load_sem.at[i])
        for i, (src, dst) in enumerate(
            [(feat_hbm, feat), (order_hbm, order), (weight_hbm, weight), (vals_hbm, vals), (cot, c_all.at[rep])]
        )
    ]
    for load in loads:
        load.start()
    enter([sibling, left, right] + row_peers)

    def block(index, h):
        return c_all.at[index, pl.ds(h * half, half)]

    for h in range(HALVES):
        own = cot.at[pl.ds(h * half, half)]

        @pl.when(place < places - 1)
        def _():
            remote(own, block(rep, h), r_send.at[0, h], r_recv.at[0, h], right).start()

        @pl.when(place > 0)
        def _():
            remote(own, block(rep, h), l_send.at[0, h], l_recv.at[0, h], left).start()

    for h in range(HALVES):
        own = cot.at[pl.ds(h * half, half)]
        remote(own, block(rep, h), f_send.at[place, h], f_recv.at[place, h], sibling).start()

    def relay(step):
        for h in range(HALVES):

            @pl.when(place >= step)
            def _():
                origin = place - step
                held = block(origin * 2 + core, h)
                remote(held, held, r_send.at[step - 1, h], r_recv.at[step - 1, h], left).wait_recv()
                if step < places - 1:

                    @pl.when(place < places - 1)
                    def _():
                        remote(held, held, r_send.at[step, h], r_recv.at[step, h], right).start()

                remote(held, held, f_send.at[origin, h], f_recv.at[origin, h], sibling).start()

            @pl.when(place + step < places)
            def _():
                origin = place + step
                held = block(origin * 2 + core, h)
                remote(held, held, l_send.at[step - 1, h], l_recv.at[step - 1, h], right).wait_recv()
                if step < places - 1:

                    @pl.when(place > 0)
                    def _():
                        remote(held, held, l_send.at[step, h], l_recv.at[step, h], left).start()

                remote(held, held, f_send.at[origin, h], f_recv.at[origin, h], sibling).start()

    for load in loads[:3]:
        load.wait()
    lane = lax.broadcasted_iota(jnp.int32, (tile, slab), 1)
    for t in range(per_slab):
        piece = order[0:1, t * tile : (t + 1) * tile]
        column = jnp.transpose(jnp.broadcast_to(piece, (tile, tile)))
        wide = jnp.concatenate([column] * per_slab, axis=1)
        pick = jnp.where(wide == lane, 1.0, 0.0).astype(BF16)
        x_all[row, pl.ds(t * tile, tile), :] = jnp.dot(
            pick, feat[...], preferred_element_type=F32
        ).astype(BF16)
    x_copies = []
    for d, peer in enumerate(row_peers, 1):
        copy = remote(x_all.at[row], x_all.at[row], x_send.at[d], x_recv.at[d], peer)
        copy.start()
        x_copies.append(copy)

    def project(owner):
        for t in range(per_slab):
            z[owner * per_slab + t] = jnp.dot(
                x_all[owner, pl.ds(t * tile, tile), :], weight[...], preferred_element_type=F32
            ).astype(BF16)

    z[n_row * per_slab] = jnp.zeros((tile, z.shape[2]), BF16)
    project(row)
    relay(1)
    for d in range(1, n_row):
        sender = lax.rem(row - d + n_row, n_row)
        remote(
            x_all.at[sender], x_all.at[sender], x_send.at[d], x_recv.at[d], (sender, rep)
        ).wait_recv()
        project(sender)
    loads[3].wait()
    if places > 2:
        relay(2)

    def block_row(r):
        count = counts[0, r]
        lhs = jnp.concatenate([vals[r, m] for m in range(slots)], axis=1)
        picked = [
            z[jnp.where(m < count, cols[0, m, r], n_row * per_slab)] for m in range(slots)
        ]
        return jnp.dot(lhs, jnp.concatenate(picked, axis=0), preferred_element_type=F32)

    def for_sibling(q, carry):
        first = (q * 2 + 1 - core) * per_slab
        for t in range(per_slab):
            to_sib[q, pl.ds(t * tile, tile), :] = block_row(first + t).astype(BF16)
        remote(to_sib.at[q], from_sib.at[q], h_send.at[q], h_recv.at[q], sibling).start()
        return carry

    lax.fori_loop(0, places, for_sibling, 0)
    if places > 3:
        relay(3)

    def for_self(q, carry):
        first = (q * 2 + core) * per_slab
        remote(to_sib.at[q], from_sib.at[q], h_send.at[q], h_recv.at[q], sibling).wait()
        for t in range(per_slab):
            rows = pl.ds(t * tile, tile)
            from_sib[q, rows, :] = (block_row(first + t) + from_sib[q, rows, :].astype(F32)).astype(BF16)
        pltpu.make_async_copy(from_sib.at[q], pair_out.at[q], p_sem.at[q]).start()
        return carry

    lax.fori_loop(0, places, for_self, 0)

    for step in range(4, places):
        relay(step)

    for q in range(places):
        pltpu.make_async_copy(from_sib.at[q], pair_out.at[q], p_sem.at[q]).wait()
        for h in range(HALVES):
            held = block(q * 2 + 1 - core, h)
            remote(held, held, f_send.at[q, h], f_recv.at[q, h], sibling).wait()
    loads[4].wait()
    for copy in x_copies:
        copy.wait_send()
    for step in range(places - 1):
        for h in range(HALVES):
            held = block(rep, h)

            @pl.when((place < places - 1) & (place >= step))
            def _():
                remote(held, held, r_send.at[step, h], r_recv.at[step, h], right).wait_send()

            @pl.when((place > 0) & (place + step < places))
            def _():
                remote(held, held, l_send.at[step, h], l_recv.at[step, h], left).wait_send()


def backward_kernel(cols, counts, vals, cot, x_all, spread, local, total):
    step = pl.program_id(0)
    rows, slots, tile = vals.shape[0], vals.shape[1], vals.shape[2]
    tiles = total.shape[0] - 1

    @pl.when(step == 0)
    def _():
        total[...] = jnp.zeros_like(total)

    for k in range(rows):
        r = step * rows + k
        count = counts[0, r]
        wide = jnp.concatenate([vals[k, m] for m in range(slots)], axis=1)
        terms = lax.dot_general(
            cot[k], wide, (((0,), (0,)), ((), ())), preferred_element_type=F32
        )
        for m in range(slots):
            at = jnp.where(m < count, cols[0, m, r], tiles)
            total[at] = total[at] + terms[:, m * tile : (m + 1) * tile]

    @pl.when(step == pl.num_programs(0) - 1)
    def _():
        acc = jnp.zeros(local.shape, F32)
        for c in range(tiles):
            at = pl.ds(c * tile, tile)
            held = total[c]
            spread[at, :] = jnp.transpose(held).astype(BF16)
            acc += jnp.dot(held.astype(BF16), x_all[at, :], preferred_element_type=F32)
        local[...] = jnp.transpose(acc)


def reduce_kernel(
    n_row, n_rep, scale, pair_hbm, spread, local, weight,
    hidden, feature_grad, weight_grad,
    pair, r_in, l_in, r_sum, l_sum, s_in, w_in, w_row,
    r_send, r_recv, l_send, l_recv, own_sem, s_send, s_recv, a_send, a_recv, b_send, b_recv, g_send, g_recv,
):
    row, rep = lax.axis_index("row"), lax.axis_index("rep")
    places = n_rep // 2
    core, place = lax.rem(rep, 2), rep // 2
    part = local.shape[0] // n_rep
    row_peers = [(lax.rem(row + d, n_row), rep) for d in range(1, n_row)]
    all_peers = [(row, lax.rem(rep + d, n_rep)) for d in range(1, n_rep)]
    right = (row, lax.rem(place + 1, places) * 2 + core)
    left = (row, lax.rem(place + places - 1, places) * 2 + core)
    half = pair.shape[1] // HALVES
    own = pltpu.make_async_copy(spread.at[row], s_in.at[row], own_sem.at[0])
    own.start()
    load = pltpu.make_async_copy(pair_hbm, pair, own_sem.at[1])
    load.start()
    enter(row_peers + all_peers)

    def piece(index):
        return pl.ds(pl.multiple_of(index * part, part), part)

    started = []

    def send(src, dst, send_sem, recv_sem, peer):
        copy = remote(src, dst, send_sem, recv_sem, peer)
        copy.start()
        started.append(copy)

    for d, peer in enumerate(all_peers, 1):
        send(local.at[piece(peer[1])], w_in.at[rep], a_send.at[d], a_recv.at[d], peer)
    def send_spread(h):
        rows = pl.ds(h * half, half)
        for d, peer in enumerate(row_peers, 1):
            send(spread.at[peer[0], rows], s_in.at[row, rows], s_send.at[d, h], s_recv.at[d, h], peer)

    send_spread(0)
    def add(held, arrived, q, rows):
        held[q, rows, :] = (arrived[q, rows, :].astype(F32) + pair[q, rows, :].astype(F32)).astype(BF16)

    def relay(step):
        to_right = places - 1 + place - step
        to_left = step - (places - 1) + place
        for h in range(HALVES):
            rows = pl.ds(h * half, half)

            @pl.when((to_right > place) & (to_right < places))
            def _():
                q = to_right
                target, sems = r_in.at[q, rows], (r_send.at[q, h], r_recv.at[q, h])

                @pl.when(place == 0)
                def _():
                    remote(pair.at[q, rows], target, *sems, right).start()

                @pl.when(place > 0)
                def _():
                    remote(target, target, *sems, left).wait_recv()
                    add(r_sum, r_in, q, rows)
                    remote(r_sum.at[q, rows], target, *sems, right).start()

            @pl.when((to_left >= 0) & (to_left < place))
            def _():
                q = to_left
                target, sems = l_in.at[q, rows], (l_send.at[q, h], l_recv.at[q, h])

                @pl.when(place == places - 1)
                def _():
                    remote(pair.at[q, rows], target, *sems, left).start()

                @pl.when(place < places - 1)
                def _():
                    remote(target, target, *sems, right).wait_recv()
                    add(l_sum, l_in, q, rows)
                    remote(l_sum.at[q, rows], target, *sems, left).start()

    load.wait()
    relay(0)
    w_in[rep] = local[piece(rep), :]
    for d in range(1, n_rep):
        sender = lax.rem(rep - d + n_rep, n_rep)
        remote(
            local.at[piece(rep)], w_in.at[sender], a_send.at[d], a_recv.at[d], (row, sender)
        ).wait_recv()
    w_row[row] = jnp.sum(w_in[...], axis=0)
    for d, peer in enumerate(row_peers, 1):
        send(w_row.at[row], w_row.at[row], b_send.at[d], b_recv.at[d], peer)
    for h in range(1, HALVES):
        send_spread(h)
    if places > 2:
        relay(1)
    for d in range(1, n_row):
        sender = lax.rem(row - d + n_row, n_row)
        remote(
            w_row.at[sender], w_row.at[sender], b_send.at[d], b_recv.at[d], (sender, rep)
        ).wait_recv()
    weight_grad[piece(rep), :] = jnp.sum(w_row[...], axis=0) * scale
    for d, peer in enumerate(all_peers, 1):
        send(
            weight_grad.at[piece(rep)], weight_grad.at[piece(rep)], g_send.at[d], g_recv.at[d], peer
        )

    for step in range(2, places - 1):
        relay(step)
    own.wait()
    grad = s_in[row].astype(F32)
    for d in range(1, n_row):
        sender = lax.rem(row - d + n_row, n_row)
        for h in range(HALVES):
            rows = pl.ds(h * half, half)
            remote(
                spread.at[row, rows], s_in.at[sender, rows], s_send.at[d, h], s_recv.at[d, h], (sender, rep)
            ).wait_recv()
        grad += s_in[sender].astype(F32)
    feature_grad[...] = lax.dot_general(
        grad.astype(BF16), weight[...], (((1,), (1,)), ((), ())), preferred_element_type=F32
    ).astype(BF16)

    for h in range(HALVES):
        rows = pl.ds(h * half, half)

        @pl.when(place > 0)
        def _():
            target = r_in.at[place, rows]
            remote(target, target, r_send.at[place, h], r_recv.at[place, h], left).wait_recv()

        @pl.when(place < places - 1)
        def _():
            target = l_in.at[place, rows]
            remote(target, target, l_send.at[place, h], l_recv.at[place, h], right).wait_recv()

        @pl.when(place == 0)
        def _():
            hidden[rows, :] = (pair[place, rows, :].astype(F32) + l_in[place, rows, :].astype(F32)).astype(BF16)

        @pl.when(place == places - 1)
        def _():
            hidden[rows, :] = (pair[place, rows, :].astype(F32) + r_in[place, rows, :].astype(F32)).astype(BF16)

        @pl.when((place > 0) & (place < places - 1))
        def _():
            hidden[rows, :] = (
                pair[place, rows, :].astype(F32)
                + r_in[place, rows, :].astype(F32)
                + l_in[place, rows, :].astype(F32)
            ).astype(BF16)

    for q in range(places):
        for h in range(HALVES):
            held = r_sum.at[q, pl.ds(h * half, half)]

            @pl.when(place < q)
            def _():
                remote(held, held, r_send.at[q, h], r_recv.at[q, h], right).wait_send()

            @pl.when(place > q)
            def _():
                remote(held, held, l_send.at[q, h], l_recv.at[q, h], left).wait_send()

    for d in range(1, n_rep):
        sender = lax.rem(rep - d + n_rep, n_rep)
        remote(
            weight_grad.at[piece(sender)], weight_grad.at[piece(sender)],
            g_send.at[d], g_recv.at[d], (row, sender),
        ).wait_recv()
    for copy in started:
        copy.wait_send()


def solution(mesh):
    n_row, n_rep = mesh.shape["row"], mesh.shape["rep"]
    places = n_rep // 2
    vmem = pl.BlockSpec(memory_space=pltpu.VMEM)
    smem = pl.BlockSpec(memory_space=pltpu.SMEM)
    hbm = pl.BlockSpec(memory_space=pltpu.HBM)
    dma = pltpu.SemaphoreType.DMA

    def shards(features, node_order, weight, tile_vals, tile_cols, row_counts, cotangent):
        slab, width = features.shape
        depth = weight.shape[1]
        tile_rows, _, slots, tile, _ = tile_vals.shape
        tiles = n_row * slab // tile
        vals = tile_vals.reshape(tile_rows, slots, tile, tile)
        cols = jnp.transpose(tile_cols, (1, 2, 0))
        counts = jnp.transpose(row_counts, (1, 0))
        shape = jax.ShapeDtypeStruct
        x_all, c_all, pair = pl.pallas_call(
            functools.partial(forward_kernel, n_row, n_rep),
            name="forward",
            out_shape=(
                shape((n_row, slab, width), BF16),
                shape((n_rep, slab, depth), BF16),
                shape((places, slab, depth), BF16),
            ),
            in_specs=[hbm, hbm, hbm, smem, smem, hbm, hbm],
            out_specs=(vmem, hbm, hbm),
            scratch_shapes=[
                pltpu.VMEM(vals.shape, BF16),
                pltpu.VMEM(features.shape, BF16),
                pltpu.VMEM(node_order.shape, jnp.int32),
                pltpu.VMEM(weight.shape, BF16),
                pltpu.VMEM((tiles + 1, tile, depth), BF16),
                pltpu.VMEM((places, slab, depth), BF16),
                pltpu.VMEM((places, slab, depth), BF16),
                dma((5,)),
                dma((n_row,)), dma((n_row,)),
                dma((places, HALVES)), dma((places, HALVES)),
                dma((places, HALVES)), dma((places, HALVES)),
                dma((places, HALVES)), dma((places, HALVES)),
                dma((places,)), dma((places,)),
                dma((places,)),
            ],
            compiler_params=pltpu.CompilerParams(
                collective_id=0, has_side_effects=True, vmem_limit_bytes=VMEM_LIMIT
            ),
        )(features, node_order, weight, cols, counts, cotangent, vals)

        chunk = 8
        spread, local = pl.pallas_call(
            backward_kernel,
            name="backward",
            grid=(tile_rows // chunk,),
            out_shape=(shape((tiles * tile, depth), BF16), shape((width, depth), F32)),
            in_specs=[
                smem, smem,
                pl.BlockSpec((chunk, slots, tile, tile), lambda i: (i, 0, 0, 0)),
                pl.BlockSpec((chunk, tile, depth), lambda i: (i, 0, 0)),
                pl.BlockSpec((tiles * tile, width), lambda i: (0, 0)),
            ],
            out_specs=(
                pl.BlockSpec((tiles * tile, depth), lambda i: (0, 0)),
                pl.BlockSpec((width, depth), lambda i: (0, 0)),
            ),
            scratch_shapes=[pltpu.VMEM((tiles + 1, depth, tile), F32)],
            compiler_params=pltpu.CompilerParams(vmem_limit_bytes=MIDDLE_LIMIT),
        )(
            cols, counts, vals,
            c_all.reshape(tile_rows, tile, depth), x_all.reshape(tiles * tile, width),
        )

        nodes = slab * n_row * n_rep
        part = width // n_rep
        return pl.pallas_call(
            functools.partial(reduce_kernel, n_row, n_rep, 1.0 / math.sqrt(nodes)),
            name="reduce",
            out_shape=(
                shape((slab, depth), BF16),
                shape((slab, width), BF16),
                shape((width, depth), F32),
            ),
            in_specs=[hbm, hbm, vmem, vmem],
            out_specs=(vmem,) * 3,
            scratch_shapes=[
                pltpu.VMEM((places, slab, depth), BF16),
                pltpu.VMEM((places, slab, depth), BF16),
                pltpu.VMEM((places, slab, depth), BF16),
                pltpu.VMEM((places, slab, depth), BF16),
                pltpu.VMEM((places, slab, depth), BF16),
                pltpu.VMEM((n_row, slab, depth), BF16),
                pltpu.VMEM((n_rep, part, depth), F32),
                pltpu.VMEM((n_row, part, depth), F32),
                dma((places, HALVES)), dma((places, HALVES)),
                dma((places, HALVES)), dma((places, HALVES)),
                dma((2,)),
                dma((n_row, HALVES)), dma((n_row, HALVES)),
                dma((n_rep,)), dma((n_rep,)),
                dma((n_row,)), dma((n_row,)),
                dma((n_rep,)), dma((n_rep,)),
            ],
            compiler_params=pltpu.CompilerParams(
                collective_id=1, has_side_effects=True, vmem_limit_bytes=LATER_LIMIT
            ),
        )(pair, spread.reshape(n_row, slab, depth), local, weight)

    return jax.shard_map(
        shards,
        mesh=mesh,
        in_specs=(
            P(("row", "rep"), None),
            P(("row", "rep"), None),
            P(),
            P("row", "rep", None, None, None),
            P("row", "rep", None),
            P("row", "rep"),
            P(("row", "rep"), None),
        ),
        out_specs=(P(("row", "rep"), None), P(("row", "rep"), None), P()),
        check_vma=False,
    )
```

```python
import functools
import math

import jax
import jax.numpy as jnp
from jax import lax
from jax.experimental import pallas as pl
from jax.experimental.pallas import tpu as pltpu
from jax.sharding import PartitionSpec as P

MESH = pl.DeviceIdType.MESH
VMEM_LIMIT = 63 * 1024 * 1024
F32 = jnp.float32
BF16 = jnp.bfloat16
MIDDLE_LIMIT = 52 * 1024 * 1024
LATER_LIMIT = 40 * 1024 * 1024
HALVES = 2


def remote(src, dst, send, recv, device):
    return pltpu.make_async_remote_copy(
        src_ref=src, dst_ref=dst, send_sem=send, recv_sem=recv, device_id=device, device_id_type=MESH
    )


def enter(devices):
    barrier = pltpu.get_barrier_semaphore()
    for device in devices:
        pl.semaphore_signal(barrier, inc=1, device_id=device, device_id_type=MESH)
    pl.semaphore_wait(barrier, len(devices))


def forward_kernel(
    n_row, n_rep, feat_hbm, order_hbm, weight_hbm, cols, counts, cot, vals_hbm,
    x_all, c_all, pair_out,
    vals, feat, order, weight, z, to_sib, from_sib, hop_in,
    load_sem, x_send, x_recv, r_send, r_recv, l_send, l_recv, f_send, f_recv, h_send, h_recv, p_sem, e_send, e_recv,
):
    row, rep = lax.axis_index("row"), lax.axis_index("rep")
    places = n_rep // 2
    core, place = lax.rem(rep, 2), rep // 2
    slab = feat.shape[0]
    half = slab // HALVES
    tile = z.shape[1]
    per_slab = slab // tile
    slots = cols.shape[1]
    sibling = (row, place * 2 + 1 - core)
    row_peers = [(lax.rem(row + d, n_row), rep) for d in range(1, n_row)]
    right = (row, lax.rem(place + 1, places) * 2 + core)
    left = (row, lax.rem(place + places - 1, places) * 2 + core)
    loads = [
        pltpu.make_async_copy(src, dst, load_sem.at[i])
        for i, (src, dst) in enumerate(
            [(feat_hbm, feat), (order_hbm, order), (weight_hbm, weight), (vals_hbm, vals), (cot, c_all.at[rep])]
        )
    ]
    for load in loads:
        load.start()
    enter([sibling, left, right] + row_peers)

    def block(index, h):
        return c_all.at[index, pl.ds(h * half, half)]

    for h in range(HALVES):
        own = cot.at[pl.ds(h * half, half)]

        @pl.when(place < places - 1)
        def _():
            remote(own, block(rep, h), r_send.at[0, h], r_recv.at[0, h], right).start()

        @pl.when(place > 0)
        def _():
            remote(own, block(rep, h), l_send.at[0, h], l_recv.at[0, h], left).start()

    for h in range(HALVES):
        own = cot.at[pl.ds(h * half, half)]
        remote(own, block(rep, h), f_send.at[place, h], f_recv.at[place, h], sibling).start()

    def relay(step):
        for h in range(HALVES):

            @pl.when(place >= step)
            def _():
                origin = place - step
                held = block(origin * 2 + core, h)
                remote(held, held, r_send.at[step - 1, h], r_recv.at[step - 1, h], left).wait_recv()
                if step < places - 1:

                    @pl.when(place < places - 1)
                    def _():
                        remote(held, held, r_send.at[step, h], r_recv.at[step, h], right).start()

                remote(held, held, f_send.at[origin, h], f_recv.at[origin, h], sibling).start()

            @pl.when(place + step < places)
            def _():
                origin = place + step
                held = block(origin * 2 + core, h)
                remote(held, held, l_send.at[step - 1, h], l_recv.at[step - 1, h], right).wait_recv()
                if step < places - 1:

                    @pl.when(place > 0)
                    def _():
                        remote(held, held, l_send.at[step, h], l_recv.at[step, h], left).start()

                remote(held, held, f_send.at[origin, h], f_recv.at[origin, h], sibling).start()

    for load in loads[:3]:
        load.wait()
    lane = lax.broadcasted_iota(jnp.int32, (tile, slab), 1)
    for t in range(per_slab):
        piece = order[0:1, t * tile : (t + 1) * tile]
        column = jnp.transpose(jnp.broadcast_to(piece, (tile, tile)))
        wide = jnp.concatenate([column] * per_slab, axis=1)
        pick = jnp.where(wide == lane, 1.0, 0.0).astype(BF16)
        x_all[row, pl.ds(t * tile, tile), :] = jnp.dot(
            pick, feat[...], preferred_element_type=F32
        ).astype(BF16)
    x_copies = []
    for d, peer in enumerate(row_peers, 1):
        copy = remote(x_all.at[row], x_all.at[row], x_send.at[d], x_recv.at[d], peer)
        copy.start()
        x_copies.append(copy)

    def project(owner):
        for t in range(per_slab):
            z[owner * per_slab + t] = jnp.dot(
                x_all[owner, pl.ds(t * tile, tile), :], weight[...], preferred_element_type=F32
            ).astype(BF16)

    z[n_row * per_slab] = jnp.zeros((tile, z.shape[2]), BF16)
    project(row)
    relay(1)
    for d in range(1, n_row):
        sender = lax.rem(row - d + n_row, n_row)
        remote(
            x_all.at[sender], x_all.at[sender], x_send.at[d], x_recv.at[d], (sender, rep)
        ).wait_recv()
        project(sender)
        if d == 1:
            relay(2)
    loads[3].wait()

    def block_row(r):
        count = counts[0, r]
        lhs = jnp.concatenate([vals[r, m] for m in range(slots)], axis=1)
        picked = [
            z[jnp.where(m < count, cols[0, m, r], n_row * per_slab)] for m in range(slots)
        ]
        return jnp.dot(lhs, jnp.concatenate(picked, axis=0), preferred_element_type=F32)

    def turn(k):
        return lax.rem(k + places - 1 - place, places)

    def for_sibling(k):
        q = turn(k)
        first = (q * 2 + 1 - core) * per_slab
        for t in range(per_slab):
            to_sib[q, pl.ds(t * tile, tile), :] = block_row(first + t).astype(BF16)
        remote(to_sib.at[q], from_sib.at[q], h_send.at[q], h_recv.at[q], sibling).start()

    def for_self(k):
        q = turn(k)
        first = (q * 2 + core) * per_slab
        remote(to_sib.at[q], from_sib.at[q], h_send.at[q], h_recv.at[q], sibling).wait()
        for t in range(per_slab):
            rows = pl.ds(t * tile, tile)
            from_sib[q, rows, :] = (block_row(first + t) + from_sib[q, rows, :].astype(F32)).astype(BF16)

        @pl.when(((place != 1) | (q != places - 1)) & ((place != places - 2) | (q != 0)))
        def _():
            pltpu.make_async_copy(from_sib.at[q], pair_out.at[q], p_sem.at[q]).start()

    def hop(side, h, q, device):
        rows = pl.ds(h * half, half)
        return remote(
            from_sib.at[q, rows], hop_in.at[side, rows], e_send.at[side, h], e_recv.at[side, h], device
        )

    for_sibling(0)
    for_sibling(1)
    for_self(0)
    for h in range(HALVES):

        @pl.when(place == 0)
        def _():
            hop(0, h, places - 1, right).start()

        @pl.when(place == places - 1)
        def _():
            hop(1, h, 0, left).start()

    def both(k, carry):
        for_sibling(k + 1)
        for_self(k)
        return carry

    lax.fori_loop(1, places - 1, both, 0)
    for_self(places - 1)
    relay(3)
    for step in range(4, places):
        relay(step)

    def land(side, q, device):
        for h in range(HALVES):
            rows = pl.ds(h * half, half)
            hop(side, h, q, device).wait_recv()
            from_sib[q, rows, :] = (
                from_sib[q, rows, :].astype(F32) + hop_in[side, rows, :].astype(F32)
            ).astype(BF16)
        pltpu.make_async_copy(from_sib.at[q], pair_out.at[q], p_sem.at[q]).start()

    @pl.when(place == 1)
    def _():
        land(0, places - 1, left)

    @pl.when(place == places - 2)
    def _():
        land(1, 0, right)

    for h in range(HALVES):

        @pl.when(place == 0)
        def _():
            hop(0, h, places - 1, right).wait_send()

        @pl.when(place == places - 1)
        def _():
            hop(1, h, 0, left).wait_send()

    for q in range(places):
        pltpu.make_async_copy(from_sib.at[q], pair_out.at[q], p_sem.at[q]).wait()
        for h in range(HALVES):
            held = block(q * 2 + 1 - core, h)
            remote(held, held, f_send.at[q, h], f_recv.at[q, h], sibling).wait()
    loads[4].wait()
    for copy in x_copies:
        copy.wait_send()
    for step in range(places - 1):
        for h in range(HALVES):
            held = block(rep, h)

            @pl.when((place < places - 1) & (place >= step))
            def _():
                remote(held, held, r_send.at[step, h], r_recv.at[step, h], right).wait_send()

            @pl.when((place > 0) & (place + step < places))
            def _():
                remote(held, held, l_send.at[step, h], l_recv.at[step, h], left).wait_send()


def backward_kernel(cols, counts, vals, cot, x_all, spread, local, total):
    step = pl.program_id(0)
    rows, slots, tile = vals.shape[0], vals.shape[1], vals.shape[2]
    tiles = total.shape[0] - 1

    @pl.when(step == 0)
    def _():
        total[...] = jnp.zeros_like(total)

    for k in range(rows):
        r = step * rows + k
        count = counts[0, r]
        wide = jnp.concatenate([vals[k, m] for m in range(slots)], axis=1)
        terms = lax.dot_general(
            cot[k], wide, (((0,), (0,)), ((), ())), preferred_element_type=F32
        )
        for m in range(slots):
            at = jnp.where(m < count, cols[0, m, r], tiles)
            total[at] = total[at] + terms[:, m * tile : (m + 1) * tile]

    @pl.when(step == pl.num_programs(0) - 1)
    def _():
        acc = jnp.zeros(local.shape, F32)
        for c in range(tiles):
            at = pl.ds(c * tile, tile)
            held = total[c]
            spread[at, :] = jnp.transpose(held).astype(BF16)
            acc += jnp.dot(held.astype(BF16), x_all[at, :], preferred_element_type=F32)
        local[...] = jnp.transpose(acc)


def reduce_kernel(
    n_row, n_rep, scale, pair_hbm, spread, local, weight,
    hidden, feature_grad, weight_grad,
    pair, r_in, l_in, r_sum, l_sum, s_in, w_in, w_row,
    r_send, r_recv, l_send, l_recv, own_sem, s_send, s_recv, a_send, a_recv, b_send, b_recv, g_send, g_recv,
):
    row, rep = lax.axis_index("row"), lax.axis_index("rep")
    places = n_rep // 2
    core, place = lax.rem(rep, 2), rep // 2
    part = local.shape[0] // n_rep
    row_peers = [(lax.rem(row + d, n_row), rep) for d in range(1, n_row)]
    all_peers = [(row, lax.rem(rep + d, n_rep)) for d in range(1, n_rep)]
    right = (row, lax.rem(place + 1, places) * 2 + core)
    left = (row, lax.rem(place + places - 1, places) * 2 + core)
    half = pair.shape[1] // HALVES
    own = pltpu.make_async_copy(spread.at[row], s_in.at[row], own_sem.at[0])
    own.start()
    load = pltpu.make_async_copy(pair_hbm, pair, own_sem.at[1])
    load.start()
    enter(row_peers + all_peers)

    def piece(index):
        return pl.ds(pl.multiple_of(index * part, part), part)

    started = []

    def send(src, dst, send_sem, recv_sem, peer):
        copy = remote(src, dst, send_sem, recv_sem, peer)
        copy.start()
        started.append(copy)

    for d, peer in enumerate(all_peers, 1):
        send(local.at[piece(peer[1])], w_in.at[rep], a_send.at[d], a_recv.at[d], peer)
    def send_spread(h):
        rows = pl.ds(h * half, half)
        for d, peer in enumerate(row_peers, 1):
            send(spread.at[peer[0], rows], s_in.at[row, rows], s_send.at[d, h], s_recv.at[d, h], peer)

    send_spread(0)
    def add(held, arrived, q, rows):
        held[q, rows, :] = (arrived[q, rows, :].astype(F32) + pair[q, rows, :].astype(F32)).astype(BF16)

    def relay(step):
        to_right = places - 2 + place - step
        to_left = place + step + 2 - places
        for h in range(HALVES):
            rows = pl.ds(h * half, half)

            @pl.when((to_right > place) & (to_right < places))
            def _():
                q = to_right
                target, sems = r_in.at[q, rows], (r_send.at[q, h], r_recv.at[q, h])

                first = (place == 0) | ((place == 1) & (q == places - 1))

                @pl.when(first)
                def _():
                    remote(pair.at[q, rows], target, *sems, right).start()

                @pl.when(jnp.logical_not(first))
                def _():
                    remote(target, target, *sems, left).wait_recv()
                    add(r_sum, r_in, q, rows)
                    remote(r_sum.at[q, rows], target, *sems, right).start()

            @pl.when((to_left >= 0) & (to_left < place))
            def _():
                q = to_left
                target, sems = l_in.at[q, rows], (l_send.at[q, h], l_recv.at[q, h])

                first = (place == places - 1) | ((place == places - 2) & (q == 0))

                @pl.when(first)
                def _():
                    remote(pair.at[q, rows], target, *sems, left).start()

                @pl.when(jnp.logical_not(first))
                def _():
                    remote(target, target, *sems, right).wait_recv()
                    add(l_sum, l_in, q, rows)
                    remote(l_sum.at[q, rows], target, *sems, left).start()

    load.wait()
    relay(0)
    w_in[rep] = local[piece(rep), :]
    for d in range(1, n_rep):
        sender = lax.rem(rep - d + n_rep, n_rep)
        remote(
            local.at[piece(rep)], w_in.at[sender], a_send.at[d], a_recv.at[d], (row, sender)
        ).wait_recv()
    w_row[row] = jnp.sum(w_in[...], axis=0)
    for d, peer in enumerate(row_peers, 1):
        send(w_row.at[row], w_row.at[row], b_send.at[d], b_recv.at[d], peer)
    for h in range(1, HALVES):
        send_spread(h)
    relay(1)
    for d in range(1, n_row):
        sender = lax.rem(row - d + n_row, n_row)
        remote(
            w_row.at[sender], w_row.at[sender], b_send.at[d], b_recv.at[d], (sender, rep)
        ).wait_recv()
    weight_grad[piece(rep), :] = jnp.sum(w_row[...], axis=0) * scale
    for d, peer in enumerate(all_peers, 1):
        send(
            weight_grad.at[piece(rep)], weight_grad.at[piece(rep)], g_send.at[d], g_recv.at[d], peer
        )

    for step in range(2, places - 2):
        relay(step)
    own.wait()
    grad = s_in[row].astype(F32)
    for d in range(1, n_row):
        sender = lax.rem(row - d + n_row, n_row)
        for h in range(HALVES):
            rows = pl.ds(h * half, half)
            remote(
                spread.at[row, rows], s_in.at[sender, rows], s_send.at[d, h], s_recv.at[d, h], (sender, rep)
            ).wait_recv()
        grad += s_in[sender].astype(F32)
    feature_grad[...] = lax.dot_general(
        grad.astype(BF16), weight[...], (((1,), (1,)), ((), ())), preferred_element_type=F32
    ).astype(BF16)

    for h in range(HALVES):
        rows = pl.ds(h * half, half)

        @pl.when(place > 0)
        def _():
            target = r_in.at[place, rows]
            remote(target, target, r_send.at[place, h], r_recv.at[place, h], left).wait_recv()

        @pl.when(place < places - 1)
        def _():
            target = l_in.at[place, rows]
            remote(target, target, l_send.at[place, h], l_recv.at[place, h], right).wait_recv()

        @pl.when(place == 0)
        def _():
            hidden[rows, :] = (pair[place, rows, :].astype(F32) + l_in[place, rows, :].astype(F32)).astype(BF16)

        @pl.when(place == places - 1)
        def _():
            hidden[rows, :] = (pair[place, rows, :].astype(F32) + r_in[place, rows, :].astype(F32)).astype(BF16)

        @pl.when((place > 0) & (place < places - 1))
        def _():
            hidden[rows, :] = (
                pair[place, rows, :].astype(F32)
                + r_in[place, rows, :].astype(F32)
                + l_in[place, rows, :].astype(F32)
            ).astype(BF16)

    for q in range(places):
        for h in range(HALVES):
            held = r_sum.at[q, pl.ds(h * half, half)]

            @pl.when((place < q) & ((place != 0) | (q != places - 1)))
            def _():
                remote(held, held, r_send.at[q, h], r_recv.at[q, h], right).wait_send()

            @pl.when((place > q) & ((place != places - 1) | (q != 0)))
            def _():
                remote(held, held, l_send.at[q, h], l_recv.at[q, h], left).wait_send()

    for d in range(1, n_rep):
        sender = lax.rem(rep - d + n_rep, n_rep)
        remote(
            weight_grad.at[piece(sender)], weight_grad.at[piece(sender)],
            g_send.at[d], g_recv.at[d], (row, sender),
        ).wait_recv()
    for copy in started:
        copy.wait_send()


def solution(mesh):
    n_row, n_rep = mesh.shape["row"], mesh.shape["rep"]
    places = n_rep // 2
    vmem = pl.BlockSpec(memory_space=pltpu.VMEM)
    smem = pl.BlockSpec(memory_space=pltpu.SMEM)
    hbm = pl.BlockSpec(memory_space=pltpu.HBM)
    dma = pltpu.SemaphoreType.DMA

    def shards(features, node_order, weight, tile_vals, tile_cols, row_counts, cotangent):
        slab, width = features.shape
        depth = weight.shape[1]
        tile_rows, _, slots, tile, _ = tile_vals.shape
        tiles = n_row * slab // tile
        vals = tile_vals.reshape(tile_rows, slots, tile, tile)
        cols = jnp.transpose(tile_cols, (1, 2, 0))
        counts = jnp.transpose(row_counts, (1, 0))
        shape = jax.ShapeDtypeStruct
        x_all, c_all, pair = pl.pallas_call(
            functools.partial(forward_kernel, n_row, n_rep),
            name="forward",
            out_shape=(
                shape((n_row, slab, width), BF16),
                shape((n_rep, slab, depth), BF16),
                shape((places, slab, depth), BF16),
            ),
            in_specs=[hbm, hbm, hbm, smem, smem, hbm, hbm],
            out_specs=(vmem, hbm, hbm),
            scratch_shapes=[
                pltpu.VMEM(vals.shape, BF16),
                pltpu.VMEM(features.shape, BF16),
                pltpu.VMEM(node_order.shape, jnp.int32),
                pltpu.VMEM(weight.shape, BF16),
                pltpu.VMEM((tiles + 1, tile, depth), BF16),
                pltpu.VMEM((places, slab, depth), BF16),
                pltpu.VMEM((places, slab, depth), BF16),
                pltpu.VMEM((2, slab, depth), BF16),
                dma((5,)),
                dma((n_row,)), dma((n_row,)),
                dma((places, HALVES)), dma((places, HALVES)),
                dma((places, HALVES)), dma((places, HALVES)),
                dma((places, HALVES)), dma((places, HALVES)),
                dma((places,)), dma((places,)),
                dma((places,)),
                dma((2, HALVES)), dma((2, HALVES)),
            ],
            compiler_params=pltpu.CompilerParams(
                collective_id=0, has_side_effects=True, vmem_limit_bytes=VMEM_LIMIT
            ),
        )(features, node_order, weight, cols, counts, cotangent, vals)

        chunk = 8
        spread, local = pl.pallas_call(
            backward_kernel,
            name="backward",
            grid=(tile_rows // chunk,),
            out_shape=(shape((tiles * tile, depth), BF16), shape((width, depth), F32)),
            in_specs=[
                smem, smem,
                pl.BlockSpec((chunk, slots, tile, tile), lambda i: (i, 0, 0, 0)),
                pl.BlockSpec((chunk, tile, depth), lambda i: (i, 0, 0)),
                pl.BlockSpec((tiles * tile, width), lambda i: (0, 0)),
            ],
            out_specs=(
                pl.BlockSpec((tiles * tile, depth), lambda i: (0, 0)),
                pl.BlockSpec((width, depth), lambda i: (0, 0)),
            ),
            scratch_shapes=[pltpu.VMEM((tiles + 1, depth, tile), F32)],
            compiler_params=pltpu.CompilerParams(vmem_limit_bytes=MIDDLE_LIMIT),
        )(
            cols, counts, vals,
            c_all.reshape(tile_rows, tile, depth), x_all.reshape(tiles * tile, width),
        )

        nodes = slab * n_row * n_rep
        part = width // n_rep
        return pl.pallas_call(
            functools.partial(reduce_kernel, n_row, n_rep, 1.0 / math.sqrt(nodes)),
            name="reduce",
            out_shape=(
                shape((slab, depth), BF16),
                shape((slab, width), BF16),
                shape((width, depth), F32),
            ),
            in_specs=[hbm, hbm, vmem, vmem],
            out_specs=(vmem,) * 3,
            scratch_shapes=[
                pltpu.VMEM((places, slab, depth), BF16),
                pltpu.VMEM((places, slab, depth), BF16),
                pltpu.VMEM((places, slab, depth), BF16),
                pltpu.VMEM((places, slab, depth), BF16),
                pltpu.VMEM((places, slab, depth), BF16),
                pltpu.VMEM((n_row, slab, depth), BF16),
                pltpu.VMEM((n_rep, part, depth), F32),
                pltpu.VMEM((n_row, part, depth), F32),
                dma((places, HALVES)), dma((places, HALVES)),
                dma((places, HALVES)), dma((places, HALVES)),
                dma((2,)),
                dma((n_row, HALVES)), dma((n_row, HALVES)),
                dma((n_rep,)), dma((n_rep,)),
                dma((n_row,)), dma((n_row,)),
                dma((n_rep,)), dma((n_rep,)),
            ],
            compiler_params=pltpu.CompilerParams(
                collective_id=1, has_side_effects=True, vmem_limit_bytes=LATER_LIMIT
            ),
        )(pair, spread.reshape(n_row, slab, depth), local, weight)

    return jax.shard_map(
        shards,
        mesh=mesh,
        in_specs=(
            P(("row", "rep"), None),
            P(("row", "rep"), None),
            P(),
            P("row", "rep", None, None, None),
            P("row", "rep", None),
            P("row", "rep"),
            P(("row", "rep"), None),
        ),
        out_specs=(P(("row", "rep"), None), P(("row", "rep"), None), P()),
        check_vma=False,
    )
```

```python
import functools
import math

import jax
import jax.numpy as jnp
from jax import lax
from jax.experimental import pallas as pl
from jax.experimental.pallas import tpu as pltpu
from jax.sharding import PartitionSpec as P

MESH = pl.DeviceIdType.MESH
VMEM_LIMIT = 63 * 1024 * 1024
F32 = jnp.float32
BF16 = jnp.bfloat16
MIDDLE_LIMIT = 53 * 1024 * 1024
LATER_LIMIT = 40 * 1024 * 1024
HALVES = 2


def remote(src, dst, send, recv, device):
    return pltpu.make_async_remote_copy(
        src_ref=src, dst_ref=dst, send_sem=send, recv_sem=recv, device_id=device, device_id_type=MESH
    )


def enter(devices):
    barrier = pltpu.get_barrier_semaphore()
    for device in devices:
        pl.semaphore_signal(barrier, inc=1, device_id=device, device_id_type=MESH)
    pl.semaphore_wait(barrier, len(devices))


def forward_kernel(
    n_row, n_rep, feat_hbm, order_hbm, weight_hbm, cols, counts, cot, vals_hbm,
    x_all, c_all, pair_out,
    vals, feat, order, weight, z, to_sib, from_sib, hop_in,
    load_sem, x_send, x_recv, r_send, r_recv, l_send, l_recv, f_send, f_recv, h_send, h_recv, p_sem, e_send, e_recv,
):
    row, rep = lax.axis_index("row"), lax.axis_index("rep")
    places = n_rep // 2
    core, place = lax.rem(rep, 2), rep // 2
    slab = feat.shape[0]
    half = slab // HALVES
    tile = z.shape[1]
    per_slab = slab // tile
    slots = cols.shape[1]
    sibling = (row, place * 2 + 1 - core)
    row_peers = [(lax.rem(row + d, n_row), rep) for d in range(1, n_row)]
    right = (row, lax.rem(place + 1, places) * 2 + core)
    left = (row, lax.rem(place + places - 1, places) * 2 + core)
    loads = [
        pltpu.make_async_copy(src, dst, load_sem.at[i])
        for i, (src, dst) in enumerate(
            [(feat_hbm, feat), (order_hbm, order), (weight_hbm, weight), (vals_hbm, vals), (cot, c_all.at[rep])]
        )
    ]
    for load in loads:
        load.start()
    enter([sibling, left, right] + row_peers)

    def block(index, h):
        return c_all.at[index, pl.ds(h * half, half)]

    for h in range(HALVES):
        own = cot.at[pl.ds(h * half, half)]

        @pl.when(place < places - 1)
        def _():
            remote(own, block(rep, h), r_send.at[0, h], r_recv.at[0, h], right).start()

        @pl.when(place > 0)
        def _():
            remote(own, block(rep, h), l_send.at[0, h], l_recv.at[0, h], left).start()

    for h in range(HALVES):
        own = cot.at[pl.ds(h * half, half)]
        remote(own, block(rep, h), f_send.at[place, h], f_recv.at[place, h], sibling).start()

    def relay(step):
        for h in range(HALVES):

            @pl.when(place >= step)
            def _():
                origin = place - step
                held = block(origin * 2 + core, h)
                remote(held, held, r_send.at[step - 1, h], r_recv.at[step - 1, h], left).wait_recv()
                if step < places - 1:

                    @pl.when(place < places - 1)
                    def _():
                        remote(held, held, r_send.at[step, h], r_recv.at[step, h], right).start()

                remote(held, held, f_send.at[origin, h], f_recv.at[origin, h], sibling).start()

            @pl.when(place + step < places)
            def _():
                origin = place + step
                held = block(origin * 2 + core, h)
                remote(held, held, l_send.at[step - 1, h], l_recv.at[step - 1, h], right).wait_recv()
                if step < places - 1:

                    @pl.when(place > 0)
                    def _():
                        remote(held, held, l_send.at[step, h], l_recv.at[step, h], left).start()

                remote(held, held, f_send.at[origin, h], f_recv.at[origin, h], sibling).start()

    for load in loads[:3]:
        load.wait()
    lane = lax.broadcasted_iota(jnp.int32, (tile, slab), 1)
    for t in range(per_slab):
        piece = order[0:1, t * tile : (t + 1) * tile]
        column = jnp.transpose(jnp.broadcast_to(piece, (tile, tile)))
        wide = jnp.concatenate([column] * per_slab, axis=1)
        pick = jnp.where(wide == lane, 1.0, 0.0).astype(BF16)
        x_all[row, pl.ds(t * tile, tile), :] = jnp.dot(
            pick, feat[...], preferred_element_type=F32
        ).astype(BF16)
    x_copies = []
    for d, peer in enumerate(row_peers, 1):
        copy = remote(x_all.at[row], x_all.at[row], x_send.at[d], x_recv.at[d], peer)
        copy.start()
        x_copies.append(copy)

    def project(owner):
        for t in range(per_slab):
            z[owner * per_slab + t] = jnp.dot(
                x_all[owner, pl.ds(t * tile, tile), :], weight[...], preferred_element_type=F32
            ).astype(BF16)

    z[n_row * per_slab] = jnp.zeros((tile, z.shape[2]), BF16)
    project(row)
    relay(1)
    for d in range(1, n_row):
        sender = lax.rem(row - d + n_row, n_row)
        remote(
            x_all.at[sender], x_all.at[sender], x_send.at[d], x_recv.at[d], (sender, rep)
        ).wait_recv()
        project(sender)
        if d == 1:
            relay(2)
    loads[3].wait()

    def block_row(r):
        count = counts[0, r]
        lhs = jnp.concatenate([vals[r, m] for m in range(slots)], axis=1)
        picked = [
            z[jnp.where(m < count, cols[0, m, r], n_row * per_slab)] for m in range(slots)
        ]
        return jnp.dot(lhs, jnp.concatenate(picked, axis=0), preferred_element_type=F32)

    def turn(k):
        return lax.rem(k + places - 1 - place, places)

    def for_sibling(k):
        q = turn(k)
        first = (q * 2 + 1 - core) * per_slab
        for t in range(per_slab):
            to_sib[q, pl.ds(t * tile, tile), :] = block_row(first + t).astype(BF16)
        remote(to_sib.at[q], from_sib.at[q], h_send.at[q], h_recv.at[q], sibling).start()

    def for_self(k):
        q = turn(k)
        first = (q * 2 + core) * per_slab
        remote(to_sib.at[q], from_sib.at[q], h_send.at[q], h_recv.at[q], sibling).wait()
        for t in range(per_slab):
            rows = pl.ds(t * tile, tile)
            from_sib[q, rows, :] = (block_row(first + t) + from_sib[q, rows, :].astype(F32)).astype(BF16)

        @pl.when(((place != 1) | (q != places - 1)) & ((place != places - 2) | (q != 0)))
        def _():
            pltpu.make_async_copy(from_sib.at[q], pair_out.at[q], p_sem.at[q]).start()

    def hop(side, h, q, device):
        rows = pl.ds(h * half, half)
        return remote(
            from_sib.at[q, rows], hop_in.at[side, rows], e_send.at[side, h], e_recv.at[side, h], device
        )

    for_sibling(0)
    for_sibling(1)
    for_self(0)
    for h in range(HALVES):

        @pl.when(place == 0)
        def _():
            hop(0, h, places - 1, right).start()

        @pl.when(place == places - 1)
        def _():
            hop(1, h, 0, left).start()

    def both(k, carry):
        for_sibling(k + 1)
        for_self(k)
        return carry

    lax.fori_loop(1, places - 1, both, 0)
    for_self(places - 1)
    relay(3)
    for step in range(4, places):
        relay(step)

    def land(side, q, device):
        for h in range(HALVES):
            rows = pl.ds(h * half, half)
            hop(side, h, q, device).wait_recv()
            from_sib[q, rows, :] = (
                from_sib[q, rows, :].astype(F32) + hop_in[side, rows, :].astype(F32)
            ).astype(BF16)
        pltpu.make_async_copy(from_sib.at[q], pair_out.at[q], p_sem.at[q]).start()

    @pl.when(place == 1)
    def _():
        land(0, places - 1, left)

    @pl.when(place == places - 2)
    def _():
        land(1, 0, right)

    for h in range(HALVES):

        @pl.when(place == 0)
        def _():
            hop(0, h, places - 1, right).wait_send()

        @pl.when(place == places - 1)
        def _():
            hop(1, h, 0, left).wait_send()

    for q in range(places):
        pltpu.make_async_copy(from_sib.at[q], pair_out.at[q], p_sem.at[q]).wait()
        for h in range(HALVES):
            held = block(q * 2 + 1 - core, h)
            remote(held, held, f_send.at[q, h], f_recv.at[q, h], sibling).wait()
    loads[4].wait()
    for copy in x_copies:
        copy.wait_send()
    for step in range(places - 1):
        for h in range(HALVES):
            held = block(rep, h)

            @pl.when((place < places - 1) & (place >= step))
            def _():
                remote(held, held, r_send.at[step, h], r_recv.at[step, h], right).wait_send()

            @pl.when((place > 0) & (place + step < places))
            def _():
                remote(held, held, l_send.at[step, h], l_recv.at[step, h], left).wait_send()


def backward_kernel(cols, counts, vals, cot, x_all, spread, local, total):
    step = pl.program_id(0)
    rows, slots, tile = vals.shape[0], vals.shape[1], vals.shape[2]
    tiles = total.shape[0] - 1

    @pl.when(step == 0)
    def _():
        total[...] = jnp.zeros_like(total)

    for k in range(rows):
        r = step * rows + k
        count = counts[0, r]
        wide = jnp.concatenate([vals[k, m] for m in range(slots)], axis=1)
        terms = lax.dot_general(
            cot[k], wide, (((0,), (0,)), ((), ())), preferred_element_type=F32
        )
        for m in range(slots):
            at = jnp.where(m < count, cols[0, m, r], tiles)
            total[at] = total[at] + terms[:, m * tile : (m + 1) * tile]

    @pl.when(step == pl.num_programs(0) - 1)
    def _():
        acc = jnp.zeros(local.shape, F32)
        for c in range(tiles):
            at = pl.ds(c * tile, tile)
            held = total[c]
            spread[at, :] = jnp.transpose(held).astype(BF16)
            acc += jnp.dot(held.astype(BF16), x_all[at, :], preferred_element_type=F32)
        local[...] = jnp.transpose(acc)


def reduce_kernel(
    n_row, n_rep, scale, pair_hbm, spread, local, weight,
    hidden, feature_grad, weight_grad,
    pair, r_in, l_in, r_sum, l_sum, s_in, w_in, w_row,
    r_send, r_recv, l_send, l_recv, own_sem, s_send, s_recv, a_send, a_recv, b_send, b_recv, g_send, g_recv,
):
    row, rep = lax.axis_index("row"), lax.axis_index("rep")
    places = n_rep // 2
    core, place = lax.rem(rep, 2), rep // 2
    part = local.shape[0] // n_rep
    row_peers = [(lax.rem(row + d, n_row), rep) for d in range(1, n_row)]
    all_peers = [(row, lax.rem(rep + d, n_rep)) for d in range(1, n_rep)]
    right = (row, lax.rem(place + 1, places) * 2 + core)
    left = (row, lax.rem(place + places - 1, places) * 2 + core)
    half = pair.shape[1] // HALVES
    own = pltpu.make_async_copy(spread.at[row], s_in.at[row], own_sem.at[0])
    own.start()
    load = pltpu.make_async_copy(pair_hbm, pair, own_sem.at[1])
    load.start()
    enter(row_peers + all_peers)

    def piece(index):
        return pl.ds(pl.multiple_of(index * part, part), part)

    started = []

    def send(src, dst, send_sem, recv_sem, peer):
        copy = remote(src, dst, send_sem, recv_sem, peer)
        copy.start()
        started.append(copy)

    for d, peer in enumerate(all_peers, 1):
        send(local.at[piece(peer[1])], w_in.at[rep], a_send.at[d], a_recv.at[d], peer)
    def send_spread(h):
        rows = pl.ds(h * half, half)
        for d, peer in enumerate(row_peers, 1):
            send(spread.at[peer[0], rows], s_in.at[row, rows], s_send.at[d, h], s_recv.at[d, h], peer)

    send_spread(0)
    def add(held, arrived, q, rows):
        held[q, rows, :] = (arrived[q, rows, :].astype(F32) + pair[q, rows, :].astype(F32)).astype(BF16)

    def relay(step):
        to_right = places - 2 + place - step
        to_left = place + step + 2 - places
        for h in range(HALVES):
            rows = pl.ds(h * half, half)

            @pl.when((to_right > place) & (to_right < places))
            def _():
                q = to_right
                target, sems = r_in.at[q, rows], (r_send.at[q, h], r_recv.at[q, h])

                first = (place == 0) | ((place == 1) & (q == places - 1))

                @pl.when(first)
                def _():
                    remote(pair.at[q, rows], target, *sems, right).start()

                @pl.when(jnp.logical_not(first))
                def _():
                    remote(target, target, *sems, left).wait_recv()
                    add(r_sum, r_in, q, rows)
                    remote(r_sum.at[q, rows], target, *sems, right).start()

            @pl.when((to_left >= 0) & (to_left < place))
            def _():
                q = to_left
                target, sems = l_in.at[q, rows], (l_send.at[q, h], l_recv.at[q, h])

                first = (place == places - 1) | ((place == places - 2) & (q == 0))

                @pl.when(first)
                def _():
                    remote(pair.at[q, rows], target, *sems, left).start()

                @pl.when(jnp.logical_not(first))
                def _():
                    remote(target, target, *sems, right).wait_recv()
                    add(l_sum, l_in, q, rows)
                    remote(l_sum.at[q, rows], target, *sems, left).start()

    load.wait()
    relay(0)
    w_in[rep] = local[piece(rep), :]
    for d in range(1, n_rep):
        sender = lax.rem(rep - d + n_rep, n_rep)
        remote(
            local.at[piece(rep)], w_in.at[sender], a_send.at[d], a_recv.at[d], (row, sender)
        ).wait_recv()
    w_row[row] = jnp.sum(w_in[...], axis=0)
    for d, peer in enumerate(row_peers, 1):
        send(w_row.at[row], w_row.at[row], b_send.at[d], b_recv.at[d], peer)
    for h in range(1, HALVES):
        send_spread(h)
    relay(1)
    for d in range(1, n_row):
        sender = lax.rem(row - d + n_row, n_row)
        remote(
            w_row.at[sender], w_row.at[sender], b_send.at[d], b_recv.at[d], (sender, rep)
        ).wait_recv()
    weight_grad[piece(rep), :] = jnp.sum(w_row[...], axis=0) * scale
    for d, peer in enumerate(all_peers, 1):
        send(
            weight_grad.at[piece(rep)], weight_grad.at[piece(rep)], g_send.at[d], g_recv.at[d], peer
        )

    for step in range(2, places - 2):
        relay(step)
    own.wait()
    grad = s_in[row].astype(F32)
    for d in range(1, n_row):
        sender = lax.rem(row - d + n_row, n_row)
        for h in range(HALVES):
            rows = pl.ds(h * half, half)
            remote(
                spread.at[row, rows], s_in.at[sender, rows], s_send.at[d, h], s_recv.at[d, h], (sender, rep)
            ).wait_recv()
        grad += s_in[sender].astype(F32)
    feature_grad[...] = lax.dot_general(
        grad.astype(BF16), weight[...], (((1,), (1,)), ((), ())), preferred_element_type=F32
    ).astype(BF16)

    for h in range(HALVES):
        rows = pl.ds(h * half, half)

        @pl.when(place > 0)
        def _():
            target = r_in.at[place, rows]
            remote(target, target, r_send.at[place, h], r_recv.at[place, h], left).wait_recv()

        @pl.when(place < places - 1)
        def _():
            target = l_in.at[place, rows]
            remote(target, target, l_send.at[place, h], l_recv.at[place, h], right).wait_recv()

        @pl.when(place == 0)
        def _():
            hidden[rows, :] = (pair[place, rows, :].astype(F32) + l_in[place, rows, :].astype(F32)).astype(BF16)

        @pl.when(place == places - 1)
        def _():
            hidden[rows, :] = (pair[place, rows, :].astype(F32) + r_in[place, rows, :].astype(F32)).astype(BF16)

        @pl.when((place > 0) & (place < places - 1))
        def _():
            hidden[rows, :] = (
                pair[place, rows, :].astype(F32)
                + r_in[place, rows, :].astype(F32)
                + l_in[place, rows, :].astype(F32)
            ).astype(BF16)

    for q in range(places):
        for h in range(HALVES):
            held = r_sum.at[q, pl.ds(h * half, half)]

            @pl.when((place < q) & ((place != 0) | (q != places - 1)))
            def _():
                remote(held, held, r_send.at[q, h], r_recv.at[q, h], right).wait_send()

            @pl.when((place > q) & ((place != places - 1) | (q != 0)))
            def _():
                remote(held, held, l_send.at[q, h], l_recv.at[q, h], left).wait_send()

    for d in range(1, n_rep):
        sender = lax.rem(rep - d + n_rep, n_rep)
        remote(
            weight_grad.at[piece(sender)], weight_grad.at[piece(sender)],
            g_send.at[d], g_recv.at[d], (row, sender),
        ).wait_recv()
    for copy in started:
        copy.wait_send()


def solution(mesh):
    n_row, n_rep = mesh.shape["row"], mesh.shape["rep"]
    places = n_rep // 2
    vmem = pl.BlockSpec(memory_space=pltpu.VMEM)
    smem = pl.BlockSpec(memory_space=pltpu.SMEM)
    hbm = pl.BlockSpec(memory_space=pltpu.HBM)
    dma = pltpu.SemaphoreType.DMA

    def shards(features, node_order, weight, tile_vals, tile_cols, row_counts, cotangent):
        slab, width = features.shape
        depth = weight.shape[1]
        tile_rows, _, slots, tile, _ = tile_vals.shape
        tiles = n_row * slab // tile
        vals = tile_vals.reshape(tile_rows, slots, tile, tile)
        cols = jnp.transpose(tile_cols, (1, 2, 0))
        counts = jnp.transpose(row_counts, (1, 0))
        shape = jax.ShapeDtypeStruct
        x_all, c_all, pair = pl.pallas_call(
            functools.partial(forward_kernel, n_row, n_rep),
            name="forward",
            out_shape=(
                shape((n_row, slab, width), BF16),
                shape((n_rep, slab, depth), BF16),
                shape((places, slab, depth), BF16),
            ),
            in_specs=[hbm, hbm, hbm, smem, smem, hbm, hbm],
            out_specs=(vmem, hbm, hbm),
            scratch_shapes=[
                pltpu.VMEM(vals.shape, BF16),
                pltpu.VMEM(features.shape, BF16),
                pltpu.VMEM(node_order.shape, jnp.int32),
                pltpu.VMEM(weight.shape, BF16),
                pltpu.VMEM((tiles + 1, tile, depth), BF16),
                pltpu.VMEM((places, slab, depth), BF16),
                pltpu.VMEM((places, slab, depth), BF16),
                pltpu.VMEM((2, slab, depth), BF16),
                dma((5,)),
                dma((n_row,)), dma((n_row,)),
                dma((places, HALVES)), dma((places, HALVES)),
                dma((places, HALVES)), dma((places, HALVES)),
                dma((places, HALVES)), dma((places, HALVES)),
                dma((places,)), dma((places,)),
                dma((places,)),
                dma((2, HALVES)), dma((2, HALVES)),
            ],
            compiler_params=pltpu.CompilerParams(
                collective_id=0, has_side_effects=True, vmem_limit_bytes=VMEM_LIMIT
            ),
        )(features, node_order, weight, cols, counts, cotangent, vals)

        chunk = 16
        spread, local = pl.pallas_call(
            backward_kernel,
            name="backward",
            grid=(tile_rows // chunk,),
            out_shape=(shape((tiles * tile, depth), BF16), shape((width, depth), F32)),
            in_specs=[
                smem, smem,
                pl.BlockSpec((chunk, slots, tile, tile), lambda i: (i, 0, 0, 0)),
                pl.BlockSpec((chunk, tile, depth), lambda i: (i, 0, 0)),
                pl.BlockSpec((tiles * tile, width), lambda i: (0, 0)),
            ],
            out_specs=(
                pl.BlockSpec((tiles * tile, depth), lambda i: (0, 0)),
                pl.BlockSpec((width, depth), lambda i: (0, 0)),
            ),
            scratch_shapes=[pltpu.VMEM((tiles + 1, depth, tile), F32)],
            compiler_params=pltpu.CompilerParams(vmem_limit_bytes=MIDDLE_LIMIT),
        )(
            cols, counts, vals,
            c_all.reshape(tile_rows, tile, depth), x_all.reshape(tiles * tile, width),
        )

        nodes = slab * n_row * n_rep
        part = width // n_rep
        return pl.pallas_call(
            functools.partial(reduce_kernel, n_row, n_rep, 1.0 / math.sqrt(nodes)),
            name="reduce",
            out_shape=(
                shape((slab, depth), BF16),
                shape((slab, width), BF16),
                shape((width, depth), F32),
            ),
            in_specs=[hbm, hbm, vmem, vmem],
            out_specs=(vmem,) * 3,
            scratch_shapes=[
                pltpu.VMEM((places, slab, depth), BF16),
                pltpu.VMEM((places, slab, depth), BF16),
                pltpu.VMEM((places, slab, depth), BF16),
                pltpu.VMEM((places, slab, depth), BF16),
                pltpu.VMEM((places, slab, depth), BF16),
                pltpu.VMEM((n_row, slab, depth), BF16),
                pltpu.VMEM((n_rep, part, depth), F32),
                pltpu.VMEM((n_row, part, depth), F32),
                dma((places, HALVES)), dma((places, HALVES)),
                dma((places, HALVES)), dma((places, HALVES)),
                dma((2,)),
                dma((n_row, HALVES)), dma((n_row, HALVES)),
                dma((n_rep,)), dma((n_rep,)),
                dma((n_row,)), dma((n_row,)),
                dma((n_rep,)), dma((n_rep,)),
            ],
            compiler_params=pltpu.CompilerParams(
                collective_id=1, has_side_effects=True, vmem_limit_bytes=LATER_LIMIT
            ),
        )(pair, spread.reshape(n_row, slab, depth), local, weight)

    return jax.shard_map(
        shards,
        mesh=mesh,
        in_specs=(
            P(("row", "rep"), None),
            P(("row", "rep"), None),
            P(),
            P("row", "rep", None, None, None),
            P("row", "rep", None),
            P("row", "rep"),
            P(("row", "rep"), None),
        ),
        out_specs=(P(("row", "rep"), None), P(("row", "rep"), None), P()),
        check_vma=False,
    )
```

```python
import functools
import math

import jax
import jax.numpy as jnp
from jax import lax
from jax.experimental import pallas as pl
from jax.experimental.pallas import tpu as pltpu
from jax.sharding import PartitionSpec as P

MESH = pl.DeviceIdType.MESH
VMEM_LIMIT = 63 * 1024 * 1024
F32 = jnp.float32
BF16 = jnp.bfloat16
MIDDLE_LIMIT = 53 * 1024 * 1024
LATER_LIMIT = 40 * 1024 * 1024
HALVES = 2


def remote(src, dst, send, recv, device):
    return pltpu.make_async_remote_copy(
        src_ref=src, dst_ref=dst, send_sem=send, recv_sem=recv, device_id=device, device_id_type=MESH
    )


def enter(devices):
    barrier = pltpu.get_barrier_semaphore()
    for device in devices:
        pl.semaphore_signal(barrier, inc=1, device_id=device, device_id_type=MESH)
    pl.semaphore_wait(barrier, len(devices))


def forward_kernel(
    n_row, n_rep, feat_hbm, order_hbm, weight_hbm, cols, counts, cot, vals_hbm,
    x_all, c_all, pair_out,
    vals, feat, order, weight, z, to_sib, from_sib, hop_in,
    load_sem, x_send, x_recv, r_send, r_recv, l_send, l_recv, f_send, f_recv, h_send, h_recv, p_sem, e_send, e_recv,
):
    row, rep = lax.axis_index("row"), lax.axis_index("rep")
    places = n_rep // 2
    core, place = lax.rem(rep, 2), rep // 2
    slab = feat.shape[0]
    half = slab // HALVES
    tile = z.shape[1]
    per_slab = slab // tile
    slots = cols.shape[1]
    sibling = (row, place * 2 + 1 - core)
    row_peers = [(lax.rem(row + d, n_row), rep) for d in range(1, n_row)]
    right = (row, lax.rem(place + 1, places) * 2 + core)
    left = (row, lax.rem(place + places - 1, places) * 2 + core)
    loads = [
        pltpu.make_async_copy(src, dst, load_sem.at[i])
        for i, (src, dst) in enumerate(
            [(feat_hbm, feat), (order_hbm, order), (weight_hbm, weight), (vals_hbm, vals), (cot, c_all.at[rep])]
        )
    ]
    for load in loads:
        load.start()
    enter([sibling, left, right] + row_peers)

    def block(index, h):
        return c_all.at[index, pl.ds(h * half, half)]

    for h in range(HALVES):
        own = cot.at[pl.ds(h * half, half)]

        @pl.when(place < places - 1)
        def _():
            remote(own, block(rep, h), r_send.at[0, h], r_recv.at[0, h], right).start()

        @pl.when(place > 0)
        def _():
            remote(own, block(rep, h), l_send.at[0, h], l_recv.at[0, h], left).start()

    for h in range(HALVES):
        own = cot.at[pl.ds(h * half, half)]
        remote(own, block(rep, h), f_send.at[place, h], f_recv.at[place, h], sibling).start()

    def relay(step):
        for h in range(HALVES):

            @pl.when(place >= step)
            def _():
                origin = place - step
                held = block(origin * 2 + core, h)
                remote(held, held, r_send.at[step - 1, h], r_recv.at[step - 1, h], left).wait_recv()
                if step < places - 1:

                    @pl.when(place < places - 1)
                    def _():
                        remote(held, held, r_send.at[step, h], r_recv.at[step, h], right).start()

                remote(held, held, f_send.at[origin, h], f_recv.at[origin, h], sibling).start()

            @pl.when(place + step < places)
            def _():
                origin = place + step
                held = block(origin * 2 + core, h)
                remote(held, held, l_send.at[step - 1, h], l_recv.at[step - 1, h], right).wait_recv()
                if step < places - 1:

                    @pl.when(place > 0)
                    def _():
                        remote(held, held, l_send.at[step, h], l_recv.at[step, h], left).start()

                remote(held, held, f_send.at[origin, h], f_recv.at[origin, h], sibling).start()

    for load in loads[:3]:
        load.wait()
    lane = lax.broadcasted_iota(jnp.int32, (tile, slab), 1)
    for t in range(per_slab):
        piece = order[0:1, t * tile : (t + 1) * tile]
        column = jnp.transpose(jnp.broadcast_to(piece, (tile, tile)))
        wide = jnp.concatenate([column] * per_slab, axis=1)
        pick = jnp.where(wide == lane, 1.0, 0.0).astype(BF16)
        x_all[row, pl.ds(t * tile, tile), :] = jnp.dot(
            pick, feat[...], preferred_element_type=F32
        ).astype(BF16)
    x_copies = []
    for d, peer in enumerate(row_peers, 1):
        copy = remote(x_all.at[row], x_all.at[row], x_send.at[d], x_recv.at[d], peer)
        copy.start()
        x_copies.append(copy)

    def project(owner):
        for t in range(per_slab):
            z[owner * per_slab + t] = jnp.dot(
                x_all[owner, pl.ds(t * tile, tile), :], weight[...], preferred_element_type=F32
            ).astype(BF16)

    z[n_row * per_slab] = jnp.zeros((tile, z.shape[2]), BF16)
    project(row)
    relay(1)
    for d in range(1, n_row):
        sender = lax.rem(row - d + n_row, n_row)
        remote(
            x_all.at[sender], x_all.at[sender], x_send.at[d], x_recv.at[d], (sender, rep)
        ).wait_recv()
        project(sender)
        if d == 1:
            relay(2)
    loads[3].wait()

    def block_row(r):
        count = counts[0, r]
        lhs = jnp.concatenate([vals[r, m] for m in range(slots)], axis=1)
        picked = [
            z[jnp.where(m < count, cols[0, m, r], n_row * per_slab)] for m in range(slots)
        ]
        return jnp.dot(lhs, jnp.concatenate(picked, axis=0), preferred_element_type=F32)

    def turn(k):
        return lax.rem(k + places - 1 - place, places)

    def for_sibling(k):
        q = turn(k)
        first = (q * 2 + 1 - core) * per_slab
        for t in range(per_slab):
            to_sib[q, pl.ds(t * tile, tile), :] = block_row(first + t).astype(BF16)
        remote(to_sib.at[q], from_sib.at[q], h_send.at[q], h_recv.at[q], sibling).start()

    def for_self(k):
        q = turn(k)
        first = (q * 2 + core) * per_slab
        remote(to_sib.at[q], from_sib.at[q], h_send.at[q], h_recv.at[q], sibling).wait()
        for t in range(per_slab):
            rows = pl.ds(t * tile, tile)
            from_sib[q, rows, :] = (block_row(first + t) + from_sib[q, rows, :].astype(F32)).astype(BF16)

        @pl.when(((place != 1) | (q != places - 1)) & ((place != places - 2) | (q != 0)))
        def _():
            pltpu.make_async_copy(from_sib.at[q], pair_out.at[q], p_sem.at[q]).start()

    def hop(side, h, q, device):
        rows = pl.ds(h * half, half)
        return remote(
            from_sib.at[q, rows], hop_in.at[side, rows], e_send.at[side, h], e_recv.at[side, h], device
        )

    for_sibling(0)
    for_sibling(1)
    for_self(0)
    for h in range(HALVES):

        @pl.when(place == 0)
        def _():
            hop(0, h, places - 1, right).start()

        @pl.when(place == places - 1)
        def _():
            hop(1, h, 0, left).start()

    def both(k, carry):
        for_sibling(k + 1)
        for_self(k)
        return carry

    lax.fori_loop(1, places - 1, both, 0)
    for_self(places - 1)
    relay(3)
    for step in range(4, places):
        relay(step)

    def land(side, q, device):
        for h in range(HALVES):
            rows = pl.ds(h * half, half)
            hop(side, h, q, device).wait_recv()
            from_sib[q, rows, :] = (
                from_sib[q, rows, :].astype(F32) + hop_in[side, rows, :].astype(F32)
            ).astype(BF16)
        pltpu.make_async_copy(from_sib.at[q], pair_out.at[q], p_sem.at[q]).start()

    @pl.when(place == 1)
    def _():
        land(0, places - 1, left)

    @pl.when(place == places - 2)
    def _():
        land(1, 0, right)

    for h in range(HALVES):

        @pl.when(place == 0)
        def _():
            hop(0, h, places - 1, right).wait_send()

        @pl.when(place == places - 1)
        def _():
            hop(1, h, 0, left).wait_send()

    for q in range(places):
        pltpu.make_async_copy(from_sib.at[q], pair_out.at[q], p_sem.at[q]).wait()
        for h in range(HALVES):
            held = block(q * 2 + 1 - core, h)
            remote(held, held, f_send.at[q, h], f_recv.at[q, h], sibling).wait()
    loads[4].wait()
    for copy in x_copies:
        copy.wait_send()
    for step in range(places - 1):
        for h in range(HALVES):
            held = block(rep, h)

            @pl.when((place < places - 1) & (place >= step))
            def _():
                remote(held, held, r_send.at[step, h], r_recv.at[step, h], right).wait_send()

            @pl.when((place > 0) & (place + step < places))
            def _():
                remote(held, held, l_send.at[step, h], l_recv.at[step, h], left).wait_send()


def backward_kernel(cols, counts, vals, cot, x_all, spread, local, total):
    step = pl.program_id(0)
    rows, slots, tile = vals.shape[0], vals.shape[1], vals.shape[2]
    tiles = total.shape[0] - 1

    @pl.when(step == 0)
    def _():
        total[...] = jnp.zeros_like(total)

    for k in range(rows):
        r = step * rows + k
        count = counts[0, r]
        wide = jnp.concatenate([vals[k, m] for m in range(slots)], axis=1)
        terms = lax.dot_general(
            cot[k], wide, (((0,), (0,)), ((), ())), preferred_element_type=F32
        )
        for m in range(slots):
            at = jnp.where(m < count, cols[0, m, r], tiles)
            total[at] = total[at] + terms[:, m * tile : (m + 1) * tile]

    @pl.when(step == pl.num_programs(0) - 1)
    def _():
        acc = jnp.zeros(local.shape, F32)
        for c in range(tiles):
            at = pl.ds(c * tile, tile)
            held = total[c]
            spread[at, :] = jnp.transpose(held).astype(BF16)
            acc += jnp.dot(held.astype(BF16), x_all[at, :], preferred_element_type=F32)
        local[...] = jnp.transpose(acc)


def reduce_kernel(
    n_row, n_rep, scale, pair_hbm, spread, local, weight,
    hidden, feature_grad, weight_grad,
    pair, r_in, l_in, r_sum, l_sum, s_in, w_in, w_row,
    r_send, r_recv, l_send, l_recv, own_sem, s_send, s_recv, a_send, a_recv, b_send, b_recv, g_send, g_recv,
):
    row, rep = lax.axis_index("row"), lax.axis_index("rep")
    places = n_rep // 2
    core, place = lax.rem(rep, 2), rep // 2
    part = local.shape[0] // n_rep
    row_peers = [(lax.rem(row + d, n_row), rep) for d in range(1, n_row)]
    all_peers = [(row, lax.rem(rep + d, n_rep)) for d in range(1, n_rep)]
    right = (row, lax.rem(place + 1, places) * 2 + core)
    left = (row, lax.rem(place + places - 1, places) * 2 + core)
    half = pair.shape[1] // HALVES
    own = pltpu.make_async_copy(spread.at[row], s_in.at[row], own_sem.at[0])
    own.start()
    load = pltpu.make_async_copy(pair_hbm, pair, own_sem.at[1])
    load.start()
    enter(row_peers + all_peers)

    def piece(index):
        return pl.ds(pl.multiple_of(index * part, part), part)

    started = []

    def send(src, dst, send_sem, recv_sem, peer):
        copy = remote(src, dst, send_sem, recv_sem, peer)
        copy.start()
        started.append(copy)

    for d, peer in enumerate(all_peers, 1):
        send(local.at[piece(peer[1])], w_in.at[rep], a_send.at[d], a_recv.at[d], peer)
    def send_spread(h):
        rows = pl.ds(h * half, half)
        for d, peer in enumerate(row_peers, 1):
            send(spread.at[peer[0], rows], s_in.at[row, rows], s_send.at[d, h], s_recv.at[d, h], peer)

    send_spread(0)
    def add(held, arrived, q, rows):
        held[q, rows, :] = (arrived[q, rows, :].astype(F32) + pair[q, rows, :].astype(F32)).astype(BF16)

    def relay(step):
        to_right = places - 2 + place - step
        to_left = place + step + 2 - places
        for h in range(HALVES):
            rows = pl.ds(h * half, half)

            @pl.when((to_right > place) & (to_right < places))
            def _():
                q = to_right
                target, sems = r_in.at[q, rows], (r_send.at[q, h], r_recv.at[q, h])

                first = (place == 0) | ((place == 1) & (q == places - 1))

                @pl.when(first)
                def _():
                    remote(pair.at[q, rows], target, *sems, right).start()

                @pl.when(jnp.logical_not(first))
                def _():
                    remote(target, target, *sems, left).wait_recv()
                    add(r_sum, r_in, q, rows)
                    remote(r_sum.at[q, rows], target, *sems, right).start()

            @pl.when((to_left >= 0) & (to_left < place))
            def _():
                q = to_left
                target, sems = l_in.at[q, rows], (l_send.at[q, h], l_recv.at[q, h])

                first = (place == places - 1) | ((place == places - 2) & (q == 0))

                @pl.when(first)
                def _():
                    remote(pair.at[q, rows], target, *sems, left).start()

                @pl.when(jnp.logical_not(first))
                def _():
                    remote(target, target, *sems, right).wait_recv()
                    add(l_sum, l_in, q, rows)
                    remote(l_sum.at[q, rows], target, *sems, left).start()

    load.wait()
    relay(0)
    w_in[rep] = local[piece(rep), :]
    for d in range(1, n_rep):
        sender = lax.rem(rep - d + n_rep, n_rep)
        remote(
            local.at[piece(rep)], w_in.at[sender], a_send.at[d], a_recv.at[d], (row, sender)
        ).wait_recv()
    w_row[row] = jnp.sum(w_in[...], axis=0)
    for d, peer in enumerate(row_peers, 1):
        send(w_row.at[row], w_row.at[row], b_send.at[d], b_recv.at[d], peer)
    for h in range(1, HALVES):
        send_spread(h)
    relay(1)
    for d in range(1, n_row):
        sender = lax.rem(row - d + n_row, n_row)
        remote(
            w_row.at[sender], w_row.at[sender], b_send.at[d], b_recv.at[d], (sender, rep)
        ).wait_recv()
    weight_grad[piece(rep), :] = jnp.sum(w_row[...], axis=0) * scale
    for d, peer in enumerate(all_peers, 1):
        send(
            weight_grad.at[piece(rep)], weight_grad.at[piece(rep)], g_send.at[d], g_recv.at[d], peer
        )

    for step in range(2, places - 2):
        relay(step)
    own.wait()
    grad = s_in[row].astype(F32)
    for d in range(1, n_row):
        sender = lax.rem(row - d + n_row, n_row)
        for h in range(HALVES):
            rows = pl.ds(h * half, half)
            remote(
                spread.at[row, rows], s_in.at[sender, rows], s_send.at[d, h], s_recv.at[d, h], (sender, rep)
            ).wait_recv()
        grad += s_in[sender].astype(F32)
    feature_grad[...] = lax.dot_general(
        grad.astype(BF16), weight[...], (((1,), (1,)), ((), ())), preferred_element_type=F32
    ).astype(BF16)

    for h in range(HALVES):
        rows = pl.ds(h * half, half)

        @pl.when(place > 0)
        def _():
            target = r_in.at[place, rows]
            remote(target, target, r_send.at[place, h], r_recv.at[place, h], left).wait_recv()

        @pl.when(place < places - 1)
        def _():
            target = l_in.at[place, rows]
            remote(target, target, l_send.at[place, h], l_recv.at[place, h], right).wait_recv()

        @pl.when(place == 0)
        def _():
            hidden[rows, :] = (pair[place, rows, :].astype(F32) + l_in[place, rows, :].astype(F32)).astype(BF16)

        @pl.when(place == places - 1)
        def _():
            hidden[rows, :] = (pair[place, rows, :].astype(F32) + r_in[place, rows, :].astype(F32)).astype(BF16)

        @pl.when((place > 0) & (place < places - 1))
        def _():
            hidden[rows, :] = (
                pair[place, rows, :].astype(F32)
                + r_in[place, rows, :].astype(F32)
                + l_in[place, rows, :].astype(F32)
            ).astype(BF16)

    for q in range(places):
        for h in range(HALVES):
            held = r_sum.at[q, pl.ds(h * half, half)]

            @pl.when((place < q) & ((place != 0) | (q != places - 1)))
            def _():
                remote(held, held, r_send.at[q, h], r_recv.at[q, h], right).wait_send()

            @pl.when((place > q) & ((place != places - 1) | (q != 0)))
            def _():
                remote(held, held, l_send.at[q, h], l_recv.at[q, h], left).wait_send()

    for d in range(1, n_rep):
        sender = lax.rem(rep - d + n_rep, n_rep)
        remote(
            weight_grad.at[piece(sender)], weight_grad.at[piece(sender)],
            g_send.at[d], g_recv.at[d], (row, sender),
        ).wait_recv()
    for copy in started:
        copy.wait_send()


def solution(mesh):
    n_row, n_rep = mesh.shape["row"], mesh.shape["rep"]
    places = n_rep // 2
    vmem = pl.BlockSpec(memory_space=pltpu.VMEM)
    smem = pl.BlockSpec(memory_space=pltpu.SMEM)
    hbm = pl.BlockSpec(memory_space=pltpu.HBM)
    dma = pltpu.SemaphoreType.DMA

    def shards(features, node_order, weight, tile_vals, tile_cols, row_counts, cotangent):
        slab, width = features.shape
        depth = weight.shape[1]
        tile_rows, _, slots, tile, _ = tile_vals.shape
        tiles = n_row * slab // tile
        vals = tile_vals.reshape(tile_rows, slots, tile, tile)
        cols = jnp.transpose(tile_cols, (1, 2, 0))
        counts = jnp.transpose(row_counts, (1, 0))
        shape = jax.ShapeDtypeStruct
        x_all, c_all, pair = pl.pallas_call(
            functools.partial(forward_kernel, n_row, n_rep),
            name="forward",
            out_shape=(
                shape((n_row, slab, width), BF16),
                shape((n_rep, slab, depth), BF16),
                shape((places, slab, depth), BF16),
            ),
            in_specs=[hbm, hbm, hbm, smem, smem, hbm, hbm],
            out_specs=(vmem, hbm, hbm),
            scratch_shapes=[
                pltpu.VMEM(vals.shape, BF16),
                pltpu.VMEM(features.shape, BF16),
                pltpu.VMEM(node_order.shape, jnp.int32),
                pltpu.VMEM(weight.shape, BF16),
                pltpu.VMEM((tiles + 1, tile, depth), BF16),
                pltpu.VMEM((places, slab, depth), BF16),
                pltpu.VMEM((places, slab, depth), BF16),
                pltpu.VMEM((2, slab, depth), BF16),
                dma((5,)),
                dma((n_row,)), dma((n_row,)),
                dma((places, HALVES)), dma((places, HALVES)),
                dma((places, HALVES)), dma((places, HALVES)),
                dma((places, HALVES)), dma((places, HALVES)),
                dma((places,)), dma((places,)),
                dma((places,)),
                dma((2, HALVES)), dma((2, HALVES)),
            ],
            compiler_params=pltpu.CompilerParams(
                collective_id=0, has_side_effects=True, vmem_limit_bytes=VMEM_LIMIT
            ),
        )(features, node_order, weight, cols, counts, cotangent, vals)

        chunk = 24
        spread, local = pl.pallas_call(
            backward_kernel,
            name="backward",
            grid=(tile_rows // chunk,),
            out_shape=(shape((tiles * tile, depth), BF16), shape((width, depth), F32)),
            in_specs=[
                smem, smem,
                pl.BlockSpec((chunk, slots, tile, tile), lambda i: (i, 0, 0, 0)),
                pl.BlockSpec((chunk, tile, depth), lambda i: (i, 0, 0)),
                pl.BlockSpec((tiles * tile, width), lambda i: (0, 0)),
            ],
            out_specs=(
                pl.BlockSpec((tiles * tile, depth), lambda i: (0, 0)),
                pl.BlockSpec((width, depth), lambda i: (0, 0)),
            ),
            scratch_shapes=[pltpu.VMEM((tiles + 1, depth, tile), F32)],
            compiler_params=pltpu.CompilerParams(vmem_limit_bytes=MIDDLE_LIMIT),
        )(
            cols, counts, vals,
            c_all.reshape(tile_rows, tile, depth), x_all.reshape(tiles * tile, width),
        )

        nodes = slab * n_row * n_rep
        part = width // n_rep
        return pl.pallas_call(
            functools.partial(reduce_kernel, n_row, n_rep, 1.0 / math.sqrt(nodes)),
            name="reduce",
            out_shape=(
                shape((slab, depth), BF16),
                shape((slab, width), BF16),
                shape((width, depth), F32),
            ),
            in_specs=[hbm, hbm, vmem, vmem],
            out_specs=(vmem,) * 3,
            scratch_shapes=[
                pltpu.VMEM((places, slab, depth), BF16),
                pltpu.VMEM((places, slab, depth), BF16),
                pltpu.VMEM((places, slab, depth), BF16),
                pltpu.VMEM((places, slab, depth), BF16),
                pltpu.VMEM((places, slab, depth), BF16),
                pltpu.VMEM((n_row, slab, depth), BF16),
                pltpu.VMEM((n_rep, part, depth), F32),
                pltpu.VMEM((n_row, part, depth), F32),
                dma((places, HALVES)), dma((places, HALVES)),
                dma((places, HALVES)), dma((places, HALVES)),
                dma((2,)),
                dma((n_row, HALVES)), dma((n_row, HALVES)),
                dma((n_rep,)), dma((n_rep,)),
                dma((n_row,)), dma((n_row,)),
                dma((n_rep,)), dma((n_rep,)),
            ],
            compiler_params=pltpu.CompilerParams(
                collective_id=1, has_side_effects=True, vmem_limit_bytes=LATER_LIMIT
            ),
        )(pair, spread.reshape(n_row, slab, depth), local, weight)

    return jax.shard_map(
        shards,
        mesh=mesh,
        in_specs=(
            P(("row", "rep"), None),
            P(("row", "rep"), None),
            P(),
            P("row", "rep", None, None, None),
            P("row", "rep", None),
            P("row", "rep"),
            P(("row", "rep"), None),
        ),
        out_specs=(P(("row", "rep"), None), P(("row", "rep"), None), P()),
        check_vma=False,
    )
```
